128 devices in a mesh: dp: 16 (over x, z_lo, core), proto: 8 (over z_hi, y).
Axes of the slice: x: 4, y: 4, z: 4 (z_hi: 2, z_lo: 2; z = z_hi * 2 + z_lo), core: 2. Of those that a mesh axis runs over, the one named last changes fastest.
Arguments:
- teacher_emb: bfloat16 [8192, 256], P('dp'), may hold values from -8 to 8
- student_emb: bfloat16 [8192, 256], P('dp'), may hold values from -8 to 8
- teacher_protos: bfloat16 [256, 65536], P(None, 'proto'), may hold values from -8 to 8
- student_protos: bfloat16 [256, 65536], P(None, 'proto'), may hold values from -8 to 8
Outputs:
- grad_embeddings: float32 [8192, 256], P(('dp', 'proto'))
- grad_prototypes: float32 [256, 65536], P('dp', 'proto')
- loss: float32 [], replicated
The draws below stay inside these ranges and needn't reach their ends.
All inputs are finite; a program needn't handle non-finite values.
Results may differ from the reference program's by a relative error of at most 0.0068.
Values sent between devices are 32-bit elements; how exact they have to be, the bound alone decides.
No kernel may reach another device: no remote copies, remote signals or barrier semaphores. Data moves between devices by JAX's collectives and lax.ppermute only.
A program may use at most 128 MiB of HBM per device.

```python
import jax
import jax.numpy as jnp
from jax import lax

D = 256
PROTO_DEV = 8192
ROWS_DEV = 512
ITERS = 3
CROPS = 8192
PROTOS = 65536


cluster_count = 16


def shared_directions(key):
    return jax.random.normal(jax.random.fold_in(key, 101), (D, cluster_count), jnp.float32)


def skewed_pick(key, count):
    picks = jax.random.randint(key, (count,), 0, 8)
    return jnp.where(picks < 4, 0, jnp.where(picks < 6, 1, jnp.where(picks < 7, 2, 3)))


def block_levels(key, count, per_block):
    blocks = count // per_block
    places = jnp.arange(blocks, dtype=jnp.float32) / max(blocks - 1, 1)
    levels = 0.6 * places + 0.4 * jax.random.uniform(key, (blocks,), jnp.float32)
    offsets = jax.random.randint(jax.random.fold_in(key, 7), (blocks,), 0, cluster_count)
    owners = jnp.arange(count) // per_block
    return (levels[owners], offsets[owners])


def proto_base(key):
    directions = shared_directions(key)
    levels, offsets = block_levels(jax.random.fold_in(key, 115), PROTOS, PROTO_DEV)
    labels = (offsets + 5 * skewed_pick(jax.random.fold_in(key, 111), PROTOS)) % cluster_count
    signs = jax.random.randint(jax.random.fold_in(key, 112), (PROTOS,), 0, 2) * 2 - 1
    strength = jnp.exp(jax.random.uniform(jax.random.fold_in(key, 113), (PROTOS,), jnp.float32, -0.8, 0.1) - 0.4 + 0.9 * levels)
    noise = jax.random.normal(jax.random.fold_in(key, 114), (D, PROTOS), jnp.float32)
    return directions[:, labels] * (signs * strength)[None, :] + 0.6 * noise


def crop_base(key):
    directions = shared_directions(key)
    levels, offsets = block_levels(jax.random.fold_in(key, 125), CROPS, ROWS_DEV)
    labels = (offsets + 3 * skewed_pick(jax.random.fold_in(key, 121), CROPS)) % cluster_count
    signs = jax.random.randint(jax.random.fold_in(key, 122), (CROPS,), 0, 2) * 2 - 1
    strength = jnp.exp(jax.random.uniform(jax.random.fold_in(key, 123), (CROPS,), jnp.float32, -0.5, 0.2) - 0.5 + levels)
    noise = jax.random.normal(jax.random.fold_in(key, 124), (CROPS, D), jnp.float32)
    values = directions[:, labels].T * (signs * strength)[:, None] + 0.5 * (0.6 + 0.8 * levels)[:, None] * noise
    return (values, levels)


def draw_teacher_emb(key, part):
    base, levels = crop_base(key)
    key = jax.random.fold_in(key, 1)
    values = base + 0.4 * jax.random.normal(key, (CROPS, D), jnp.float32)
    return jnp.clip(values, -8.0, 8.0).astype(jnp.bfloat16)


def draw_student_emb(key, part):
    base, levels = crop_base(key)
    key = jax.random.fold_in(key, 2)
    amount = (0.6 * (1.3 - levels))[:, None]
    values = base + amount * jax.random.normal(key, (CROPS, D), jnp.float32)
    return jnp.clip(values, -8.0, 8.0).astype(jnp.bfloat16)


def draw_teacher_protos(key, part):
    base = proto_base(key)
    key = jax.random.fold_in(key, 3)
    values = base + 0.2 * jax.random.normal(key, (D, PROTOS), jnp.float32)
    return jnp.clip(values, -8.0, 8.0).astype(jnp.bfloat16)


def draw_student_protos(key, part):
    base = proto_base(key)
    key = jax.random.fold_in(key, 4)
    values = base + 0.3 * jax.random.normal(key, (D, PROTOS), jnp.float32)
    return jnp.clip(values, -8.0, 8.0).astype(jnp.bfloat16)


def setup_inputs(seed: int = 0) -> dict:
    seeds = jax.random.split(jax.random.key(seed), 5)
    return {
        "teacher_emb": draw_teacher_emb(jax.random.fold_in(seeds[4], 71), 0),
        "student_emb": draw_student_emb(jax.random.fold_in(seeds[4], 71), 0),
        "teacher_protos": draw_teacher_protos(jax.random.fold_in(seeds[4], 71), 0),
        "student_protos": draw_student_protos(jax.random.fold_in(seeds[4], 71), 0),
    }


teacher_temp = 0.07
student_temp = 0.1
norm_eps = 1e-06

def unit_rows(values):
    wide = values.astype(jnp.float32)
    norms = jnp.sqrt(lax.optimization_barrier(jnp.sum(wide * wide, axis=1, keepdims=True)) + norm_eps)
    return (wide / norms, norms)

def unit_cols(values):
    wide = values.astype(jnp.float32)
    norms = jnp.sqrt(lax.optimization_barrier(jnp.sum(wide * wide, axis=0, keepdims=True)) + norm_eps)
    return (wide / norms, norms)

def rounded(values):
    narrow = lax.optimization_barrier(values.astype(jnp.bfloat16))
    return narrow.astype(jnp.float32)

def reference(teacher_emb, student_emb, teacher_protos, student_protos):
    batch_total = teacher_emb.shape[0]
    proto_total = teacher_protos.shape[1]
    width = teacher_emb.shape[1]
    t_unit, t_norm = unit_rows(teacher_emb)
    t_round = rounded(t_unit)
    s_unit, s_norm = unit_rows(student_emb)
    s_round = rounded(s_unit)
    t_dir, t_vnorm = unit_cols(teacher_protos)
    t_wn = rounded(t_dir)
    s_dir, v_norm = unit_cols(student_protos)
    s_wn = rounded(s_dir)
    block_rows = min(1024, batch_total)
    block_count = batch_total // block_rows
    t_blocks = t_round.reshape(block_count, block_rows, width)
    s_blocks = s_round.reshape(block_count, block_rows, width)

    def teacher_block(rows):
        scores = jnp.dot(rows, t_wn, preferred_element_type=jnp.float32, precision=lax.Precision.HIGHEST)
        return jnp.exp(scores / teacher_temp)
    row_scale = jnp.ones((block_count, block_rows), jnp.float32)
    column_scale = jnp.zeros((proto_total,), jnp.float32)
    row_sum = jnp.ones((block_count, block_rows), jnp.float32)
    for sweep in range(ITERS):

        def add_cols(total, pair):
            rows, scale = pair
            return (total + lax.optimization_barrier(jnp.sum(teacher_block(rows) * scale[:, None], axis=0)), None)
        column_sum, unused = lax.scan(add_cols, jnp.zeros((proto_total,), jnp.float32), (t_blocks, row_scale))
        column_scale = 1.0 / (proto_total * column_sum)
        row_sum = lax.map(lambda rows: lax.optimization_barrier(jnp.sum(teacher_block(rows) * column_scale[None, :], axis=1)), t_blocks)
        row_scale = 1.0 / (batch_total * row_sum)

    def final_block(carry, triple):
        loss_sum, grad_wn = carry
        t_rows, s_rows, sums = triple
        targets = teacher_block(t_rows) * column_scale[None, :] / sums[:, None]
        cosine = jnp.dot(s_rows, s_wn, preferred_element_type=jnp.float32, precision=lax.Precision.HIGHEST)
        logits = cosine / student_temp
        student_exp = jnp.exp(logits)
        totals = lax.optimization_barrier(jnp.sum(student_exp, axis=1))
        log_total = jnp.log(totals)
        loss_sum = loss_sum + jnp.sum(targets * (log_total[:, None] - logits))
        grad_logits = rounded(student_exp / totals[:, None] - targets)
        grad_unit = jnp.dot(grad_logits, s_wn.T, preferred_element_type=jnp.float32, precision=lax.Precision.HIGHEST) / student_temp
        grad_wn = grad_wn + jnp.dot(s_rows.T, grad_logits, preferred_element_type=jnp.float32, precision=lax.Precision.HIGHEST) / student_temp
        return ((loss_sum, grad_wn), grad_unit)
    start_carry = (jnp.zeros((), jnp.float32), jnp.zeros((width, proto_total), jnp.float32))
    (loss_sum, grad_wn), grad_units = lax.scan(final_block, start_carry, (t_blocks, s_blocks, row_sum))
    grad_unit = grad_units.reshape(batch_total, width)
    grad_embeddings = (grad_unit - s_unit * lax.optimization_barrier(jnp.sum(s_unit * grad_unit, axis=1, keepdims=True))) / s_norm
    dots = lax.optimization_barrier(jnp.sum(s_wn * grad_wn, axis=0, keepdims=True))
    grad_prototypes = (grad_wn - s_wn * dots) / v_norm
    loss = loss_sum / batch_total
    return (grad_embeddings, grad_prototypes, loss)
```

```python
import math

import jax
import jax.numpy as jnp
from jax import lax
from jax.experimental import pallas as pl
from jax.experimental.pallas import tpu as pltpu
from jax.sharding import Mesh
from jax.sharding import PartitionSpec as P

teacher_temp = 0.07
student_temp = 0.1
norm_eps = 1e-06
log2_e = math.log2(math.e)
teacher_rate = log2_e / teacher_temp
student_rate = log2_e / student_temp

BF16 = jnp.bfloat16
F32 = jnp.float32
LANES = 128
MIB = 1 << 20


def params(mib):
    return pltpu.CompilerParams(vmem_limit_bytes=mib * MIB)


def unit_rows(wide):
    norms = jnp.sqrt(jnp.sum(wide * wide, axis=1, keepdims=True) + norm_eps)
    return wide / norms, norms


def unit_cols(wide):
    norms = jnp.sqrt(jnp.sum(wide * wide, axis=0, keepdims=True) + norm_eps)
    return (wide * (1.0 / norms)).astype(BF16), norms


def dot_rows(left, right):
    return lax.dot_general(left, right, (((1,), (1,)), ((), ())), preferred_element_type=F32)


def dot_cols(left, right):
    return lax.dot_general(left, right, (((0,), (0,)), ((), ())), preferred_element_type=F32)


def dot(left, right):
    return jnp.dot(left, right, preferred_element_type=F32)


def fold_lanes(values):
    total = values[:, :LANES]
    for first in range(LANES, values.shape[1], LANES):
        total = total + values[:, first : first + LANES]
    return total


def row_to_lanes(values):
    return jnp.sum(values.T, axis=0, keepdims=True)


def lanes_to_rows(values):
    return jnp.broadcast_to(values, (LANES, values.shape[1])).T


def place_pair(scratch, core, own, other):
    rows = own.shape[0]
    scratch[pl.ds(pl.multiple_of(core * rows, rows), rows), :] = own
    scratch[pl.ds(pl.multiple_of((1 - core) * rows, rows), rows), :] = other


def teacher_kernel(place, own, other, protos, expo, col_part, unit):
    @pl.when(pl.program_id(0) == 0)
    def _():
        first = unit_rows(own[...].astype(F32))[0].astype(BF16)
        second = unit_rows(other[...])[0].astype(BF16)
        place_pair(unit, place[0], first, second)

    directions, _ = unit_cols(protos[...].astype(F32))
    values = jnp.exp2(dot(unit[...], directions) * teacher_rate)
    expo[...] = values.astype(BF16)
    total = jnp.sum(values, axis=0, keepdims=True)
    col_part[...] = jnp.broadcast_to(total[None], col_part.shape)


def teacher_call(place, own, both, protos, copies, blocks=8):
    rows, width = own.shape
    cols = protos.shape[1] // 2
    step = cols // blocks
    return pl.pallas_call(
        teacher_kernel,
        grid_spec=pltpu.PrefetchScalarGridSpec(
            num_scalar_prefetch=1,
            grid=(blocks,),
            in_specs=[
                pl.BlockSpec((rows, width), lambda j, place: (0, 0)),
                pl.BlockSpec((rows, width), lambda j, place: (0, 0)),
                pl.BlockSpec((width, step), lambda j, place: (0, place[0] * blocks + j)),
            ],
            out_specs=[
                pl.BlockSpec((2 * rows, step), lambda j, place: (0, j)),
                pl.BlockSpec((copies, 1, step), lambda j, place: (0, 0, j)),
            ],
            scratch_shapes=[pltpu.VMEM((2 * rows, width), BF16)],
        ),
        out_shape=[
            jax.ShapeDtypeStruct((2 * rows, cols), BF16),
            jax.ShapeDtypeStruct((copies, 1, cols), F32),
        ],
        compiler_params=params(40),
        cost_estimate=pl.CostEstimate(
            flops=4 * rows * cols * width,
            bytes_accessed=2 * 2 * rows * cols + 2 * width * cols,
            transcendentals=2 * rows * cols,
        ),
        name="teacher_expo",
    )(place, own, both, protos)


def student_kernel(place, own, other, protos, mixed, total_part, dirs, round_out, unit, sums):
    step = pl.program_id(0)

    @pl.when(step == 0)
    def _():
        first = unit_rows(own[...].astype(F32))[0].astype(BF16)
        second = unit_rows(other[...])[0].astype(BF16)
        place_pair(unit, place[0], first, second)
        round_out[...] = unit[...]
        sums[...] = jnp.zeros_like(sums)
        mixed[...] = jnp.zeros_like(mixed)

    directions, _ = unit_cols(protos[...].astype(F32))
    dirs[...] = directions
    values = jnp.exp2(dot(unit[...], directions) * student_rate)
    sums[...] += fold_lanes(values)
    mixed[...] += dot_rows(values.astype(BF16), directions)

    @pl.when(step == pl.num_programs(0) - 1)
    def _():
        total_part[...] = row_to_lanes(sums[...])


def student_call(place, own, both, protos, blocks=8):
    rows, width = own.shape
    cols = protos.shape[1] // 2
    step = cols // blocks
    return pl.pallas_call(
        student_kernel,
        grid_spec=pltpu.PrefetchScalarGridSpec(
            num_scalar_prefetch=1,
            grid=(blocks,),
            in_specs=[
                pl.BlockSpec((rows, width), lambda j, place: (0, 0)),
                pl.BlockSpec((rows, width), lambda j, place: (0, 1)),
                pl.BlockSpec((width, step), lambda j, place: (0, place[0] * blocks + j)),
            ],
            out_specs=[
                pl.BlockSpec((2 * rows, width), lambda j, place: (0, 0)),
                pl.BlockSpec((1, 2 * rows), lambda j, place: (0, 0)),
                pl.BlockSpec((width, step), lambda j, place: (0, j)),
                pl.BlockSpec((2 * rows, width), lambda j, place: (0, 0)),
            ],
            scratch_shapes=[
                pltpu.VMEM((2 * rows, width), BF16),
                pltpu.VMEM((2 * rows, LANES), F32),
            ],
        ),
        out_shape=[
            jax.ShapeDtypeStruct((2 * rows, width), F32),
            jax.ShapeDtypeStruct((1, 2 * rows), F32),
            jax.ShapeDtypeStruct((width, cols), BF16),
            jax.ShapeDtypeStruct((2 * rows, width), BF16),
        ],
        compiler_params=params(40),
        cost_estimate=pl.CostEstimate(
            flops=8 * rows * cols * width,
            bytes_accessed=4 * width * cols + 8 * rows * width,
            transcendentals=2 * rows * cols,
        ),
        name="student_totals",
    )(place, own, both, protos)


def row_sweep_kernel(proto_total, col_parts, expo, row_part):
    scale = 1.0 / (proto_total * jnp.sum(col_parts[...], axis=0))
    rows, cols = expo.shape
    for first in range(0, rows, LANES):
        total = jnp.zeros((LANES, LANES), F32)
        for at in range(0, cols, LANES):
            block = expo[first : first + LANES, at : at + LANES].astype(F32)
            total = total + block * scale[:, at : at + LANES]
        sums = row_to_lanes(total)
        row_part[:, :, first : first + LANES] = jnp.broadcast_to(
            sums[None], (row_part.shape[0], 1, LANES)
        )


def row_sweep(proto_total, col_parts, expo, copies, blocks=4):
    rows, cols = expo.shape
    step = rows // blocks
    return pl.pallas_call(
        lambda *refs: row_sweep_kernel(proto_total, *refs),
        grid=(blocks,),
        in_specs=[
            pl.BlockSpec(col_parts.shape, lambda i: (0, 0, 0)),
            pl.BlockSpec((step, cols), lambda i: (i, 0)),
        ],
        out_specs=pl.BlockSpec((copies, 1, step), lambda i: (0, 0, i)),
        out_shape=jax.ShapeDtypeStruct((copies, 1, rows), F32),
        compiler_params=params(32),
        cost_estimate=pl.CostEstimate(
            flops=2 * rows * cols, bytes_accessed=2 * rows * cols, transcendentals=0
        ),
        name="row_sweep",
    )(col_parts, expo)


def col_sweep_kernel(batch_total, row_parts, expo, col_part, scale):
    @pl.when(pl.program_id(0) == 0)
    def _():
        sums = jnp.sum(row_parts[...], axis=0)
        scale[...] = lanes_to_rows(1.0 / (batch_total * sums))

    rows, cols = expo.shape
    for at in range(0, cols, LANES):
        block = expo[:, at : at + LANES].astype(F32) * scale[...]
        total = jnp.sum(block, axis=0, keepdims=True)
        col_part[:, :, at : at + LANES] = jnp.broadcast_to(
            total[None], (col_part.shape[0], 1, LANES)
        )


def col_sweep(batch_total, row_parts, expo, copies, blocks=4):
    rows, cols = expo.shape
    step = cols // blocks
    return pl.pallas_call(
        lambda *refs: col_sweep_kernel(batch_total, *refs),
        grid=(blocks,),
        in_specs=[
            pl.BlockSpec((row_parts.shape[0], 1, rows), lambda j: (0, 0, 0)),
            pl.BlockSpec((rows, step), lambda j: (0, j)),
        ],
        out_specs=pl.BlockSpec((copies, 1, step), lambda j: (0, 0, j)),
        out_shape=jax.ShapeDtypeStruct((copies, 1, cols), F32),
        scratch_shapes=[pltpu.VMEM((rows, LANES), F32)],
        compiler_params=params(32),
        cost_estimate=pl.CostEstimate(
            flops=2 * rows * cols, bytes_accessed=2 * rows * cols, transcendentals=0
        ),
        name="col_sweep",
    )(row_parts, expo)


def last_sweep_kernel(proto_total, col_parts, expo, dirs, unit, row_part, mixed, scale_out, scaled):
    scale = 1.0 / (proto_total * jnp.sum(col_parts[...], axis=0))

    @pl.when(pl.program_id(0) == 0)
    def _():
        scale_out[...] = scale
        scaled[...] = (dirs[...].astype(F32) * scale).astype(BF16)

    rows, cols = expo.shape
    copies = row_part.shape[0]
    product = dot_rows(expo[...], scaled[...])
    mixed[...] = product
    meet = fold_lanes(product * unit[...].astype(F32))
    row_part[:, 1:2, :] = jnp.broadcast_to(row_to_lanes(meet)[None], (copies, 1, rows))
    for first in range(0, rows, LANES):
        total = jnp.zeros((LANES, LANES), F32)
        for at in range(0, cols, LANES):
            block = expo[first : first + LANES, at : at + LANES].astype(F32)
            total = total + block * scale[:, at : at + LANES]
        sums = row_to_lanes(total)
        row_part[:, 0:1, first : first + LANES] = jnp.broadcast_to(
            sums[None], (copies, 1, LANES)
        )


def last_sweep(proto_total, col_parts, expo, dirs, unit, copies, blocks=4):
    rows, cols = expo.shape
    width = dirs.shape[0]
    step = rows // blocks
    return pl.pallas_call(
        lambda *refs: last_sweep_kernel(proto_total, *refs),
        grid=(blocks,),
        in_specs=[
            pl.BlockSpec((col_parts.shape[0], 1, cols), lambda i: (0, 0, 0)),
            pl.BlockSpec((step, cols), lambda i: (i, 0)),
            pl.BlockSpec((width, cols), lambda i: (0, 0)),
            pl.BlockSpec((step, width), lambda i: (i, 0)),
        ],
        out_specs=[
            pl.BlockSpec((copies, 2, step), lambda i: (0, 0, i)),
            pl.BlockSpec((step, width), lambda i: (i, 0)),
            pl.BlockSpec((1, cols), lambda i: (0, 0)),
        ],
        out_shape=[
            jax.ShapeDtypeStruct((copies, 2, rows), F32),
            jax.ShapeDtypeStruct((rows, width), F32),
            jax.ShapeDtypeStruct((1, cols), F32),
        ],
        scratch_shapes=[pltpu.VMEM((width, cols), BF16)],
        compiler_params=params(40),
        cost_estimate=pl.CostEstimate(
            flops=2 * rows * cols * (width + 1),
            bytes_accessed=2 * rows * cols + 2 * width * cols,
            transcendentals=0,
        ),
        name="last_sweep",
    )(col_parts, expo, dirs, unit)


def wide_kernel(
    place, both, totals, t_protos, s_protos, expo, rounded, dirs, col_norm, mixed, t_dirs
):
    step = pl.program_id(0)

    @pl.when(step == 0)
    def _():
        t_dirs[...] = unit_cols(t_protos[...].astype(F32))[0]
        dirs[...], col_norm[...] = unit_cols(s_protos[...].astype(F32))
        mixed[...] = jnp.zeros_like(mixed)

    width = t_dirs.shape[0]
    t_unit = unit_rows(both[:, :width])[0].astype(BF16)
    expo[...] = jnp.exp2(dot(t_unit, t_dirs[...]) * teacher_rate).astype(BF16)
    s_unit = unit_rows(both[:, width:])[0].astype(BF16)
    rounded[...] = s_unit
    log_total = lanes_to_rows(jnp.log2(totals[0]))
    shift = jnp.concatenate([log_total] * (dirs.shape[1] // LANES), axis=1)
    chance = jnp.exp2(dot(s_unit, dirs[...]) * student_rate - shift).astype(BF16)
    mixed[...] += dot_cols(s_unit, chance)


def wide_call(place, both, totals, t_protos, s_protos, parts):
    crops, double = both.shape
    width = double // 2
    rows = crops // parts
    cols = t_protos.shape[1] // parts
    whole = lambda i, place: (0, 0)
    return pl.pallas_call(
        wide_kernel,
        grid_spec=pltpu.PrefetchScalarGridSpec(
            num_scalar_prefetch=1,
            grid=(parts,),
            in_specs=[
                pl.BlockSpec((rows, double), lambda i, place: (i, 0)),
                pl.BlockSpec((1, 1, rows), lambda i, place: (i, 0, 0)),
                pl.BlockSpec((width, cols), lambda i, place: (0, place[1])),
                pl.BlockSpec((width, cols), lambda i, place: (0, place[1])),
            ],
            out_specs=[
                pl.BlockSpec((rows, cols), lambda i, place: (i, 0)),
                pl.BlockSpec((rows, width), lambda i, place: (i, 0)),
                pl.BlockSpec((width, cols), whole),
                pl.BlockSpec((1, cols), whole),
                pl.BlockSpec((width, cols), whole),
            ],
            scratch_shapes=[pltpu.VMEM((width, cols), BF16)],
        ),
        out_shape=[
            jax.ShapeDtypeStruct((crops, cols), BF16),
            jax.ShapeDtypeStruct((crops, width), BF16),
            jax.ShapeDtypeStruct((width, cols), BF16),
            jax.ShapeDtypeStruct((1, cols), F32),
            jax.ShapeDtypeStruct((width, cols), F32),
        ],
        compiler_params=params(40),
        cost_estimate=pl.CostEstimate(
            flops=6 * crops * cols * width,
            bytes_accessed=4 * crops * double + 2 * crops * cols,
            transcendentals=2 * crops * cols,
        ),
        name="wide_products",
    )(place, both, totals, t_protos, s_protos)


def finish_kernel(place, row_sums, expo, rounded, scale, dirs, mixed, keep, send, dots, total):
    step = pl.program_id(0)

    @pl.when(step == 0)
    def _():
        total[...] = jnp.zeros_like(total)

    per = row_sums.shape[2]
    parts = []
    for k in range(row_sums.shape[0]):
        inverse = lanes_to_rows(1.0 / row_sums[k])
        inverse = jnp.concatenate([inverse] * (rounded.shape[1] // LANES), axis=1)
        parts.append((rounded[k * per : (k + 1) * per, :].astype(F32) * inverse).astype(BF16))
    total[...] += dot_cols(jnp.concatenate(parts, axis=0), expo[...])

    @pl.when(step == pl.num_programs(0) - 1)
    def _():
        grad = (mixed[...] - scale[...] * total[...]) * (1.0 / student_temp)
        dots[...] = jnp.sum(grad * dirs[...].astype(F32), axis=0, keepdims=True)
        total[...] = grad
        chunks, rows = keep.shape[0], keep.shape[1]
        for k in range(chunks):
            first = pl.multiple_of((2 * k + place[0]) * rows, rows)
            other = pl.multiple_of((2 * k + 1 - place[0]) * rows, rows)
            keep[k] = total[pl.ds(first, rows), :]
            send[k] = total[pl.ds(other, rows), :]


def finish_call(place, row_sums, expo, rounded, scale, dirs, mixed, blocks=4):
    crops, cols = expo.shape
    width = dirs.shape[0]
    parts = row_sums.shape[0]
    rows = crops // blocks
    whole = lambda i, place: (0, 0)
    chunk = (parts, width // (2 * parts), cols)
    return pl.pallas_call(
        finish_kernel,
        grid_spec=pltpu.PrefetchScalarGridSpec(
            num_scalar_prefetch=1,
            grid=(blocks,),
            in_specs=[
                pl.BlockSpec((parts // blocks, 1, crops // parts), lambda i, place: (i, 0, 0)),
                pl.BlockSpec((rows, cols), lambda i, place: (i, 0)),
                pl.BlockSpec((rows, width), lambda i, place: (i, 0)),
                pl.BlockSpec((1, cols), whole),
                pl.BlockSpec((width, cols), whole),
                pl.BlockSpec((width, cols), whole),
            ],
            out_specs=[
                pl.BlockSpec(chunk, lambda i, place: (0, 0, 0)),
                pl.BlockSpec(chunk, lambda i, place: (0, 0, 0)),
                pl.BlockSpec((1, cols), whole),
            ],
            scratch_shapes=[pltpu.VMEM((width, cols), F32)],
        ),
        out_shape=[
            jax.ShapeDtypeStruct(chunk, F32),
            jax.ShapeDtypeStruct(chunk, F32),
            jax.ShapeDtypeStruct((1, cols), F32),
        ],
        compiler_params=params(40),
        cost_estimate=pl.CostEstimate(
            flops=2 * crops * cols * width,
            bytes_accessed=2 * crops * cols + 2 * crops * width,
            transcendentals=0,
        ),
        name="finish_protos",
    )(place, row_sums, expo, rounded, scale, dirs, mixed)


COL_AXES = ("x", "zl")
ROW_AXES = ("c", "zh", "y")
SWAP = [(0, 1), (1, 0)]


def exchange(values, axes):
    return lax.all_to_all(values, axes, 0, 0, tiled=True)


def swap_cores(values):
    return lax.ppermute(values, "c", SWAP)


def in_core_order(core, own, other, axis):
    first = jnp.where(core == 0, own, other)
    second = jnp.where(core == 0, other, own)
    return jnp.concatenate([first, second], axis=axis)


def on_device(teacher_emb, student_emb, teacher_protos, student_protos):
    core = lax.axis_index("c")
    chip = lax.axis_index(COL_AXES)
    group = lax.axis_index(("zh", "y"))
    chips = lax.axis_size(COL_AXES)
    groups = lax.axis_size(("zh", "y"))
    row_copies = 2 * groups
    crops, width = teacher_emb.shape
    batch_total = crops * chips * 2
    proto_total = teacher_protos.shape[1] * groups
    place = jnp.stack([core, chip]).astype(jnp.int32)

    both = jnp.concatenate([teacher_emb, student_emb], axis=1).astype(F32)
    other = swap_cores(both)
    gathered = lax.all_gather(both, COL_AXES, axis=0, tiled=True)

    expo, col_part = teacher_call(place, teacher_emb, other, teacher_protos, chips)
    student_mixed, total_part, dirs, unit = student_call(
        place, student_emb, other, student_protos
    )

    row_parts = exchange(row_sweep(proto_total, exchange(col_part, COL_AXES), expo, row_copies), ROW_AXES)
    col_parts = exchange(col_sweep(batch_total, row_parts, expo, chips), COL_AXES)
    row_part = row_sweep(proto_total, col_parts, expo, row_copies)
    total_copies = jnp.broadcast_to(total_part[None], row_part.shape)
    row_parts = exchange(jnp.concatenate([row_part, total_copies], axis=2), ROW_AXES)
    totals = jnp.sum(row_parts[:, 0, 2 * crops :], axis=0)
    col_part = col_sweep(batch_total, row_parts, expo, chips)
    own_totals = lax.dynamic_slice_in_dim(totals, core * crops, crops, 0)
    total_copies = jnp.broadcast_to(own_totals[None, None], (chips, 1, crops))
    col_parts = exchange(jnp.concatenate([col_part, total_copies], axis=2), COL_AXES)
    all_totals = col_parts[:, :, col_part.shape[2] :]
    row_part, teacher_mixed, scale = last_sweep(
        proto_total, col_parts, expo, dirs, unit, row_copies
    )
    row_parts = jnp.sum(exchange(row_part, ROW_AXES), axis=0)
    row_sum = row_parts[0]
    loss_part = jnp.sum(jnp.log(totals) - row_parts[1] / (student_temp * row_sum))

    own_sums = lax.dynamic_slice_in_dim(row_sum, core * crops, crops, 0)
    message = jnp.concatenate([own_sums, jnp.full((LANES,), loss_part, F32)])
    message = exchange(jnp.broadcast_to(message, (chips, 1, crops + LANES)), COL_AXES)
    loss = jnp.sum(message[:, 0, crops]) / batch_total

    wide_expo, wide_round, wide_dirs, wide_norm, wide_mixed = wide_call(
        place, gathered, all_totals, teacher_protos, student_protos, chips
    )
    cols = wide_expo.shape[1]
    full_scale = in_core_order(core, scale, swap_cores(scale), 1)
    wide_scale = lax.dynamic_slice_in_dim(full_scale, chip * cols, cols, 1)
    keep, send, dots_part = finish_call(
        place, message[:, :, :crops], wide_expo, wide_round, wide_scale, wide_dirs, wide_mixed
    )
    grad_rows = keep + swap_cores(send)
    dots = dots_part + swap_cores(dots_part)
    own_dirs = lax.dynamic_index_in_dim(
        wide_dirs.reshape(chips, 2, width // (2 * chips), cols), core, 1, keepdims=False
    )
    grad_rows = (grad_rows - own_dirs.astype(F32) * dots) / wide_norm
    grad_rows = exchange(grad_rows, COL_AXES)
    grad_prototypes = jnp.swapaxes(grad_rows, 0, 1).reshape(grad_rows.shape[1], chips * cols)

    crop_part = (student_mixed / totals[:, None] - teacher_mixed / row_sum[:, None]) / student_temp
    own_part = lax.dynamic_slice_in_dim(crop_part, core * crops, crops, 0)
    other_part = lax.dynamic_slice_in_dim(crop_part, (1 - core) * crops, crops, 0)
    own_part = own_part + swap_cores(other_part)
    rows = crops // groups
    parts = exchange(own_part.reshape(groups, rows, width), ("zh", "y"))
    grad_unit = jnp.sum(parts, axis=0)
    own_emb = lax.dynamic_slice_in_dim(student_emb, group * rows, rows, 0)
    s_unit, s_norm = unit_rows(own_emb.astype(F32))
    along = jnp.sum(s_unit * grad_unit, axis=1, keepdims=True)
    grad_embeddings = (grad_unit - s_unit * along) / s_norm
    return (grad_embeddings, grad_prototypes, loss)


def solution(mesh):
    fine = Mesh(mesh.devices.reshape(4, 2, 2, 2, 4), ("x", "zl", "c", "zh", "y"))
    crops, protos = ("x", "zl", "c"), ("zh", "y")
    return jax.shard_map(
        on_device,
        mesh=fine,
        in_specs=(P(crops, None), P(crops, None), P(None, protos), P(None, protos)),
        out_specs=(P(crops + protos, None), P(crops, protos), P()),
        check_vma=False,
    )
```

```python
import math

import jax
import jax.numpy as jnp
from jax import lax
from jax.experimental import pallas as pl
from jax.experimental.pallas import tpu as pltpu
from jax.sharding import Mesh
from jax.sharding import PartitionSpec as P

teacher_temp = 0.07
student_temp = 0.1
norm_eps = 1e-06
log2_e = math.log2(math.e)
teacher_rate = log2_e / teacher_temp
student_rate = log2_e / student_temp

BF16 = jnp.bfloat16
F32 = jnp.float32
LANES = 128
BLOCK = 512
MIB = 1 << 20


def params(mib):
    return pltpu.CompilerParams(vmem_limit_bytes=mib * MIB)


def unit_rows(wide):
    norms = jnp.sqrt(jnp.sum(wide * wide, axis=1, keepdims=True) + norm_eps)
    return wide / norms, norms


def unit_cols(wide):
    norms = jnp.sqrt(jnp.sum(wide * wide, axis=0, keepdims=True) + norm_eps)
    return (wide * (1.0 / norms)).astype(BF16), norms


def dot_rows(left, right):
    return lax.dot_general(left, right, (((1,), (1,)), ((), ())), preferred_element_type=F32)


def dot_cols(left, right):
    return lax.dot_general(left, right, (((0,), (0,)), ((), ())), preferred_element_type=F32)


def dot(left, right):
    return jnp.dot(left, right, preferred_element_type=F32)


def fold_lanes(values):
    total = values[:, :LANES]
    for first in range(LANES, values.shape[1], LANES):
        total = total + values[:, first : first + LANES]
    return total


def row_to_lanes(values):
    return jnp.sum(values.T, axis=0, keepdims=True)


def lanes_to_rows(values):
    return jnp.broadcast_to(values, (LANES, values.shape[1])).T


def place_pair(scratch, core, own, other):
    rows = own.shape[0]
    scratch[pl.ds(pl.multiple_of(core * rows, rows), rows), :] = own
    scratch[pl.ds(pl.multiple_of((1 - core) * rows, rows), rows), :] = other

VMEM = pl.BlockSpec(memory_space=pltpu.VMEM)
SMEM = pl.BlockSpec(memory_space=pltpu.SMEM)


def tall(values, copies):
    return jnp.broadcast_to(values[None], (copies,) + values.shape)


def teacher_kernel(place, own, other, protos, expo, col_part, unit):
    core = place[0]
    first = unit_rows(own[...].astype(F32))[0].astype(BF16)
    second = unit_rows(other[...])[0].astype(BF16)
    place_pair(unit, core, first, second)
    half = expo.shape[1]
    copies = col_part.shape[0]

    def block(j, carry):
        here = pl.ds(pl.multiple_of(j * BLOCK, BLOCK), BLOCK)
        there = pl.ds(pl.multiple_of(core * half + j * BLOCK, BLOCK), BLOCK)
        directions, _ = unit_cols(protos[:, there].astype(F32))
        values = jnp.exp2(dot(unit[...], directions) * teacher_rate)
        expo[:, here] = values.astype(BF16)
        col_part[:, :, here] = tall(jnp.sum(values, axis=0, keepdims=True), copies)
        return carry

    lax.fori_loop(0, half // BLOCK, block, 0)


def teacher_call(place, own, other, protos, copies):
    rows, width = own.shape
    cols = protos.shape[1] // 2
    return pl.pallas_call(
        teacher_kernel,
        in_specs=[SMEM, VMEM, VMEM, VMEM],
        out_specs=[VMEM, VMEM],
        out_shape=[
            jax.ShapeDtypeStruct((2 * rows, cols), BF16),
            jax.ShapeDtypeStruct((copies, 1, cols), F32),
        ],
        scratch_shapes=[pltpu.VMEM((2 * rows, width), BF16)],
        compiler_params=params(16),
        cost_estimate=pl.CostEstimate(
            flops=4 * rows * cols * width,
            bytes_accessed=2 * 2 * rows * cols + 2 * width * cols,
            transcendentals=2 * rows * cols,
        ),
        name="teacher_expo",
    )(place, own, other, protos)


def student_kernel(place, own, other, protos, mixed, total_part, dirs, unit, sums):
    core = place[0]
    first = unit_rows(own[...].astype(F32))[0].astype(BF16)
    second = unit_rows(other[...])[0].astype(BF16)
    place_pair(unit, core, first, second)
    sums[...] = jnp.zeros_like(sums)
    mixed[...] = jnp.zeros_like(mixed)
    half = dirs.shape[1]

    def block(j, carry):
        here = pl.ds(pl.multiple_of(j * BLOCK, BLOCK), BLOCK)
        there = pl.ds(pl.multiple_of(core * half + j * BLOCK, BLOCK), BLOCK)
        directions, _ = unit_cols(protos[:, there].astype(F32))
        dirs[:, here] = directions
        values = jnp.exp2(dot(unit[...], directions) * student_rate)
        sums[...] += fold_lanes(values)
        mixed[...] += dot_rows(values.astype(BF16), directions)
        return carry

    lax.fori_loop(0, half // BLOCK, block, 0)
    total_part[...] = row_to_lanes(sums[...])


def student_call(place, own, other, protos):
    rows, width = own.shape
    cols = protos.shape[1] // 2
    return pl.pallas_call(
        student_kernel,
        in_specs=[SMEM, VMEM, VMEM, VMEM],
        out_specs=[VMEM] * 4,
        out_shape=[
            jax.ShapeDtypeStruct((2 * rows, width), F32),
            jax.ShapeDtypeStruct((1, 2 * rows), F32),
            jax.ShapeDtypeStruct((width, cols), BF16),
            jax.ShapeDtypeStruct((2 * rows, width), BF16),
        ],
        scratch_shapes=[pltpu.VMEM((2 * rows, LANES), F32)],
        compiler_params=params(16),
        cost_estimate=pl.CostEstimate(
            flops=8 * rows * cols * width,
            bytes_accessed=4 * width * cols + 8 * rows * width,
            transcendentals=2 * rows * cols,
        ),
        name="student_totals",
    )(place, own, other, protos)


def row_sweep_kernel(proto_total, col_parts, expo, *rest):
    row_part, scale = rest[-2:]
    copies = row_part.shape[0]
    cols = expo.shape[1]
    sums = jnp.sum(col_parts[:, :, :cols], axis=0)
    scale[...] = jnp.broadcast_to(1.0 / (proto_total * sums), scale.shape)
    for first in range(0, expo.shape[0], LANES):
        here = slice(first, first + LANES)
        total = jnp.zeros((LANES, LANES), F32)
        for at in range(0, cols, LANES):
            wide = jnp.concatenate([scale[:, at : at + LANES]] * (LANES // 8), axis=0)
            total = total + expo[here, at : at + LANES].astype(F32) * wide
        row_part[:, 0:1, here] = tall(row_to_lanes(total), copies)
    if len(rest) > 2:
        row_part[:, 1:2, :] = tall(rest[0][...], copies)


def row_sweep(proto_total, col_parts, expo, copies, extra=()):
    rows, cols = expo.shape
    return pl.pallas_call(
        lambda *refs: row_sweep_kernel(proto_total, *refs),
        in_specs=[VMEM] * (2 + len(extra)),
        out_specs=VMEM,
        out_shape=jax.ShapeDtypeStruct((copies, 1 + len(extra), rows), F32),
        scratch_shapes=[pltpu.VMEM((8, cols), F32)],
        compiler_params=params(16),
        cost_estimate=pl.CostEstimate(
            flops=2 * rows * cols, bytes_accessed=2 * rows * cols, transcendentals=0
        ),
        name="row_sweep",
    )(col_parts, expo, *extra)


def col_sweep_kernel(batch_total, row_parts, expo, col_part, scale):
    sums = jnp.sum(row_parts[...], axis=0)
    scale[...] = lanes_to_rows(1.0 / (batch_total * sums[0:1]))
    copies = col_part.shape[0]
    cols = expo.shape[1]
    for at in range(0, cols, LANES):
        block = expo[:, at : at + LANES].astype(F32) * scale[...]
        col_part[:, :, at : at + LANES] = tall(jnp.sum(block, axis=0, keepdims=True), copies)
    if sums.shape[0] > 1:
        col_part[:, :, cols:] = tall(sums[1:2], copies)


def col_sweep(batch_total, row_parts, expo, copies):
    rows, cols = expo.shape
    extra = rows * (row_parts.shape[1] - 1)
    return pl.pallas_call(
        lambda *refs: col_sweep_kernel(batch_total, *refs),
        in_specs=[VMEM] * 2,
        out_specs=VMEM,
        out_shape=jax.ShapeDtypeStruct((copies, 1, cols + extra), F32),
        scratch_shapes=[pltpu.VMEM((rows, LANES), F32)],
        compiler_params=params(16),
        cost_estimate=pl.CostEstimate(
            flops=2 * rows * cols, bytes_accessed=2 * rows * cols, transcendentals=0
        ),
        name="col_sweep",
    )(row_parts, expo)


def last_sweep_kernel(proto_total, col_parts, expo, dirs, unit, row_part, mixed, scale_out, scaled):
    rows, cols = expo.shape
    copies = row_part.shape[0]
    scale = 1.0 / (proto_total * jnp.sum(col_parts[:, :, :cols], axis=0))
    scale_out[...] = jnp.broadcast_to(scale, scale_out.shape)
    scaled[...] = (dirs[...].astype(F32) * scale).astype(BF16)
    step = 2 * LANES

    def block(i, carry):
        here = pl.ds(pl.multiple_of(i * step, step), step)
        values = expo[here, :]
        product = dot_rows(values, scaled[...])
        mixed[here, :] = product
        meet = fold_lanes(product * unit[here, :].astype(F32))
        total = jnp.zeros((step, LANES), F32)
        for at in range(0, cols, LANES):
            wide = jnp.concatenate([scale_out[:, at : at + LANES]] * (step // 8), axis=0)
            total = total + values[:, at : at + LANES].astype(F32) * wide
        row_part[:, 0:1, here] = tall(row_to_lanes(total), copies)
        row_part[:, 1:2, here] = tall(row_to_lanes(meet), copies)
        return carry

    lax.fori_loop(0, rows // step, block, 0)


def last_sweep(proto_total, col_parts, expo, dirs, unit, copies):
    rows, cols = expo.shape
    width = dirs.shape[0]
    return pl.pallas_call(
        lambda *refs: last_sweep_kernel(proto_total, *refs),
        in_specs=[VMEM] * 4,
        out_specs=[VMEM] * 3,
        out_shape=[
            jax.ShapeDtypeStruct((copies, 2, rows), F32),
            jax.ShapeDtypeStruct((rows, width), F32),
            jax.ShapeDtypeStruct((8, cols), F32),
        ],
        scratch_shapes=[pltpu.VMEM((width, cols), BF16)],
        compiler_params=params(16),
        cost_estimate=pl.CostEstimate(
            flops=2 * rows * cols * (width + 1),
            bytes_accessed=2 * rows * cols + 2 * width * cols,
            transcendentals=0,
        ),
        name="last_sweep",
    )(col_parts, expo, dirs, unit)


def message_kernel(place, row_parts, col_parts, message):
    rows = row_parts.shape[2]
    sums = jnp.sum(row_parts[...], axis=0)
    cols = col_parts.shape[2] - rows
    totals = col_parts[place[1], :, cols:]
    inverse = 1.0 / sums[0:1]
    terms = jnp.log(totals) - sums[1:2] * inverse * (1.0 / student_temp)
    loss = jnp.sum(terms, axis=1, keepdims=True)
    message[:, :, :rows] = tall(sums[0:1], message.shape[0])
    message[:, :, rows:] = jnp.broadcast_to(loss[None], (message.shape[0], 1, LANES))


def message_call(place, row_parts, col_parts, copies):
    rows = row_parts.shape[2]
    return pl.pallas_call(
        message_kernel,
        in_specs=[SMEM, VMEM, VMEM],
        out_specs=VMEM,
        out_shape=jax.ShapeDtypeStruct((copies, 1, rows + LANES), F32),
        compiler_params=params(16),
        name="row_message",
    )(place, row_parts, col_parts)


def crop_kernel(place, row_parts, col_parts, student, teacher, own, other):
    rows, width = student.shape
    sums = jnp.sum(row_parts[:, 0:1, :], axis=0)
    totals = col_parts[place[1], :, col_parts.shape[2] - rows :]
    half = rows // 2
    factor = 1.0 / student_temp
    a = lanes_to_rows(factor / totals)
    b = lanes_to_rows(factor / sums)
    a = jnp.concatenate([a] * (width // LANES), axis=1)
    b = jnp.concatenate([b] * (width // LANES), axis=1)
    full = student[...] * a - teacher[...] * b
    swap = place[0] == 1
    own[...] = jnp.where(swap, full[half:], full[:half])
    other[...] = jnp.where(swap, full[:half], full[half:])


def crop_call(place, row_parts, col_parts, student, teacher):
    rows, width = student.shape
    return pl.pallas_call(
        crop_kernel,
        in_specs=[SMEM] + [VMEM] * 4,
        out_specs=[VMEM] * 2,
        out_shape=[jax.ShapeDtypeStruct((rows // 2, width), F32)] * 2,
        compiler_params=params(16),
        cost_estimate=pl.CostEstimate(
            flops=4 * rows * width, bytes_accessed=12 * rows * width, transcendentals=0
        ),
        name="crop_gradients",
    )(place, row_parts, col_parts, student, teacher)


def wide_kernel(place, crops, totals, protos, rounded, dirs, col_norm, mixed):
    @pl.when(pl.program_id(0) == 0)
    def _():
        dirs[...], col_norm[...] = unit_cols(protos[...].astype(F32))
        mixed[...] = jnp.zeros_like(mixed)

    unit = unit_rows(crops[...])[0].astype(BF16)
    rounded[...] = unit
    log_total = lanes_to_rows(jnp.log2(totals[0]))
    shift = jnp.concatenate([log_total] * (dirs.shape[1] // LANES), axis=1)
    chance = jnp.exp2(dot(unit, dirs[...]) * student_rate - shift).astype(BF16)
    mixed[...] += dot_cols(unit, chance)


def wide_call(place, gathered, col_parts, protos, shares):
    crops, width = gathered.shape
    chips = col_parts.shape[0]
    rows = crops // chips
    cols = protos.shape[1] // shares
    last = col_parts.shape[2] // rows - 1
    whole = lambda i, place: (0, 0)
    return pl.pallas_call(
        wide_kernel,
        grid_spec=pltpu.PrefetchScalarGridSpec(
            num_scalar_prefetch=1,
            grid=(chips,),
            in_specs=[
                pl.BlockSpec((rows, width), lambda i, place: (i, 0)),
                pl.BlockSpec((1, 1, rows), lambda i, place: (i, 0, last)),
                pl.BlockSpec((width, cols), lambda i, place: (0, place[2])),
            ],
            out_specs=[
                pl.BlockSpec((rows, width), lambda i, place: (i, 0)),
                pl.BlockSpec((width, cols), whole),
                pl.BlockSpec((1, cols), whole),
                pl.BlockSpec((width, cols), whole),
            ],
        ),
        out_shape=[
            jax.ShapeDtypeStruct((crops, width), BF16),
            jax.ShapeDtypeStruct((width, cols), BF16),
            jax.ShapeDtypeStruct((1, cols), F32),
            jax.ShapeDtypeStruct((width, cols), F32),
        ],
        compiler_params=params(48),
        cost_estimate=pl.CostEstimate(
            flops=4 * crops * cols * width,
            bytes_accessed=6 * crops * width,
            transcendentals=crops * cols,
        ),
        name="wide_products",
    )(place, gathered, col_parts, protos)


def finish_kernel(place, crops, row_sums, protos, rounded, scale, dirs, col_norm, mixed, grad, t_dirs, total):
    step = pl.program_id(0)

    @pl.when(step == 0)
    def _():
        t_dirs[...] = unit_cols(protos[...].astype(F32))[0]
        total[...] = jnp.zeros_like(total)

    unit = unit_rows(crops[...])[0].astype(BF16)
    expo = jnp.exp2(dot(unit, t_dirs[...]) * teacher_rate).astype(BF16)
    inverse = lanes_to_rows(1.0 / row_sums[0])
    inverse = jnp.concatenate([inverse] * (rounded.shape[1] // LANES), axis=1)
    weighted = (rounded[...].astype(F32) * inverse).astype(BF16)
    total[...] += dot_cols(weighted, expo)

    @pl.when(step == pl.num_programs(0) - 1)
    def _():
        values = (mixed[...] - scale[0:1] * total[...]) * (1.0 / student_temp)
        wide = dirs[...].astype(F32)
        dots = jnp.sum(values * wide, axis=0, keepdims=True)
        values = (values - wide * dots) / col_norm[...]
        grad[...] = values.reshape(grad.shape)


def finish_call(place, gathered, message, protos, rounded, scale, dirs, col_norm, mixed, shares):
    crops, width = gathered.shape
    chips = message.shape[0]
    rows = crops // chips
    cols = dirs.shape[1]
    whole = lambda i, place: (0, 0)
    return pl.pallas_call(
        finish_kernel,
        grid_spec=pltpu.PrefetchScalarGridSpec(
            num_scalar_prefetch=1,
            grid=(chips,),
            in_specs=[
                pl.BlockSpec((rows, width), lambda i, place: (i, 0)),
                pl.BlockSpec((1, 1, rows), lambda i, place: (i, 0, 0)),
                pl.BlockSpec((width, cols), lambda i, place: (0, place[2])),
                pl.BlockSpec((rows, width), lambda i, place: (i, 0)),
                pl.BlockSpec((8, cols), lambda i, place: (0, place[3])),
                pl.BlockSpec((width, cols), whole),
                pl.BlockSpec((1, cols), whole),
                pl.BlockSpec((width, cols), whole),
            ],
            out_specs=pl.BlockSpec((shares, width // shares, cols), lambda i, place: (0, 0, 0)),
            scratch_shapes=[pltpu.VMEM((width, cols), BF16), pltpu.VMEM((width, cols), F32)],
        ),
        out_shape=jax.ShapeDtypeStruct((shares, width // shares, cols), F32),
        compiler_params=params(58),
        cost_estimate=pl.CostEstimate(
            flops=4 * crops * cols * width,
            bytes_accessed=6 * crops * width,
            transcendentals=crops * cols,
        ),
        name="finish_protos",
    )(place, gathered, message, protos, rounded, scale, dirs, col_norm, mixed)


COL_AXES = ("x", "zl")
ROW_AXES = ("c", "zh", "y")
CROP_AXES = ("x", "zl", "c")
SWAP = [(0, 1), (1, 0)]


def exchange(values, axes):
    return lax.all_to_all(values, axes, 0, 0, tiled=True)


def swap_cores(values):
    return lax.ppermute(values, "c", SWAP)


def on_device(teacher_emb, student_emb, teacher_protos, student_protos):
    core = lax.axis_index("c")
    chip = lax.axis_index(COL_AXES)
    group = lax.axis_index(("zh", "y"))
    chips = lax.axis_size(COL_AXES)
    groups = lax.axis_size(("zh", "y"))
    row_copies = 2 * groups
    shares = 2 * chips
    crops, width = teacher_emb.shape
    batch_total = crops * shares
    proto_total = teacher_protos.shape[1] * groups
    share = 2 * chip + core
    place = jnp.stack([core, chip, share, share % chips]).astype(jnp.int32)

    teacher_wide = teacher_emb.astype(F32)
    teacher_other = swap_cores(teacher_wide)
    student_wide = student_emb.astype(F32)
    student_other = swap_cores(student_wide)
    student_all = lax.all_gather(student_wide, CROP_AXES, axis=0, tiled=True)
    teacher_all = lax.all_gather(teacher_wide, CROP_AXES, axis=0, tiled=True)

    expo, col_part = teacher_call(place, teacher_emb, teacher_other, teacher_protos, chips)
    student_mixed, total_part, dirs, unit = student_call(
        place, student_emb, student_other, student_protos
    )

    col_parts = exchange(col_part, COL_AXES)
    row_part = row_sweep(proto_total, col_parts, expo, row_copies)
    row_parts = exchange(row_part, ROW_AXES)
    col_part = col_sweep(batch_total, row_parts, expo, chips)
    col_parts = exchange(col_part, COL_AXES)
    row_part = row_sweep(proto_total, col_parts, expo, row_copies, (total_part,))
    row_parts = exchange(row_part, ROW_AXES)
    col_part = col_sweep(batch_total, row_parts, expo, chips)
    col_parts = exchange(col_part, COL_AXES)
    row_part, teacher_mixed, scale = last_sweep(
        proto_total, col_parts, expo, dirs, unit, row_copies
    )
    row_parts = exchange(row_part, ROW_AXES)

    message = exchange(message_call(place, row_parts, col_parts, chips), COL_AXES)
    loss = jnp.sum(message[:, 0, 2 * crops]) / batch_total

    own_part, other_part = crop_call(place, row_parts, col_parts, student_mixed, teacher_mixed)
    own_part = own_part + swap_cores(other_part)
    rows = crops // groups
    parts = exchange(own_part.reshape(groups, rows, width), ("zh", "y"))
    grad_unit = jnp.sum(parts, axis=0)
    own_emb = lax.dynamic_slice_in_dim(student_emb, group * rows, rows, 0)
    s_unit, s_norm = unit_rows(own_emb.astype(F32))
    along = jnp.sum(s_unit * grad_unit, axis=1, keepdims=True)
    grad_embeddings = (grad_unit - s_unit * along) / s_norm

    rounded, wide_dirs, wide_norm, wide_mixed = wide_call(
        place, student_all, col_parts, student_protos, shares
    )
    other_scale = swap_cores(scale)
    own_half = share // chips == core
    wide_scale = jnp.where(own_half, scale, other_scale)
    grad_rows = finish_call(
        place, teacher_all, message, teacher_protos, rounded, wide_scale,
        wide_dirs, wide_norm, wide_mixed, shares,
    )
    grad_rows = exchange(grad_rows, CROP_AXES)
    grad_prototypes = jnp.swapaxes(grad_rows, 0, 1).reshape(grad_rows.shape[1], -1)
    return (grad_embeddings, grad_prototypes, loss)


def solution(mesh):
    fine = Mesh(mesh.devices.reshape(4, 2, 2, 2, 4), ("x", "zl", "c", "zh", "y"))
    crops, protos = ("x", "zl", "c"), ("zh", "y")
    return jax.shard_map(
        on_device,
        mesh=fine,
        in_specs=(P(crops, None), P(crops, None), P(None, protos), P(None, protos)),
        out_specs=(P(crops + protos, None), P(crops, protos), P()),
        check_vma=False,
    )
```

```python
import math

import jax
import jax.numpy as jnp
from jax import lax
from jax.experimental import pallas as pl
from jax.experimental.pallas import tpu as pltpu
from jax.sharding import Mesh
from jax.sharding import PartitionSpec as P

teacher_temp = 0.07
student_temp = 0.1
norm_eps = 1e-06
log2_e = math.log2(math.e)
teacher_rate = log2_e / teacher_temp
student_rate = log2_e / student_temp

BF16 = jnp.bfloat16
F32 = jnp.float32
LANES = 128
BLOCK = 512
MIB = 1 << 20


PARAMS = pltpu.CompilerParams(vmem_limit_bytes=61 * MIB)
HELD = pltpu.CompilerParams(vmem_limit_bytes=20 * MIB)


def unit_rows(wide):
    norms = jnp.sqrt(jnp.sum(wide * wide, axis=1, keepdims=True) + norm_eps)
    return wide * (1.0 / norms), norms


def unit_cols(wide):
    norms = jnp.sqrt(jnp.sum(wide * wide, axis=0, keepdims=True) + norm_eps)
    return (wide * (1.0 / norms)).astype(BF16), norms


def dot_rows(left, right):
    return lax.dot_general(left, right, (((1,), (1,)), ((), ())), preferred_element_type=F32)


def dot_cols(left, right):
    return lax.dot_general(left, right, (((0,), (0,)), ((), ())), preferred_element_type=F32)


def dot(left, right):
    return jnp.dot(left, right, preferred_element_type=F32)


def fold_lanes(values):
    total = values[:, :LANES]
    for first in range(LANES, values.shape[1], LANES):
        total = total + values[:, first : first + LANES]
    return total


def row_to_lanes(values):
    return jnp.sum(values.T, axis=0, keepdims=True)


def lanes_to_rows(values):
    return jnp.broadcast_to(values, (LANES, values.shape[1])).T


VMEM = pl.BlockSpec(memory_space=pltpu.VMEM)
SMEM = pl.BlockSpec(memory_space=pltpu.SMEM)
HBM = pl.BlockSpec(memory_space=pltpu.HBM)
TOKEN = (8, LANES)


def whole(shape):
    return pl.BlockSpec(shape, lambda *_: (0,) * len(shape))


def tall(values, copies):
    return jnp.broadcast_to(values[None], (copies,) + values.shape)


def unit_kernel(teacher, student, teacher_unit, student_unit, both, place):
    width = teacher.shape[1]
    first = unit_rows(teacher[...].astype(F32))[0].astype(BF16).astype(F32)
    second = unit_rows(student[...].astype(F32))[0].astype(BF16).astype(F32)
    teacher_unit[...] = first
    student_unit[...] = second
    both[:, :width] = first
    both[:, width:] = second
    core, x, near = (lax.axis_index(axis) for axis in ("c", "x", "zl"))
    share = 2 * x + core
    here = (share // 4 == core).astype(jnp.int32)
    for i, value in enumerate((core, 2 * x + near, share, share % 4, near, x, here)):
        place[i] = value.astype(jnp.int32)


def unit_call(teacher, student):
    rows, width = teacher.shape
    return pl.pallas_call(
        unit_kernel,
        grid=(1,),
        in_specs=[whole((rows, width))] * 2,
        out_specs=[whole((rows, width))] * 2 + [whole((rows, 2 * width)), SMEM],
        out_shape=[
            jax.ShapeDtypeStruct((rows, width), F32),
            jax.ShapeDtypeStruct((rows, width), F32),
            jax.ShapeDtypeStruct((rows, 2 * width), F32),
            jax.ShapeDtypeStruct((7,), jnp.int32),
        ],
        compiler_params=HELD,
        name="unit_rows",
    )(teacher, student)


def pair_rows(core, own, other):
    swap = core == 1
    first = jnp.where(swap, other, own).astype(BF16)
    second = jnp.where(swap, own, other).astype(BF16)
    return jnp.concatenate([first, second], axis=0)


def teacher_kernel(place, own, other, protos, expo, col_part, unit):
    unit[...] = pair_rows(place[0], own[...], other[...])
    for first in range(0, protos.shape[1], BLOCK):
        here = slice(first, first + BLOCK)
        directions, _ = unit_cols(protos[:, here].astype(F32))
        values = jnp.exp2(dot(unit[...], directions) * teacher_rate)
        expo[:, here] = values.astype(BF16)
        col_part[:, :, here] = tall(jnp.sum(values, axis=0, keepdims=True), col_part.shape[0])


def teacher_call(place, own, other, protos, copies):
    rows, width = own.shape
    cols = protos.shape[1]
    return pl.pallas_call(
        teacher_kernel,
        in_specs=[SMEM, VMEM, VMEM, VMEM],
        out_specs=[VMEM, VMEM],
        out_shape=[
            jax.ShapeDtypeStruct((2 * rows, cols), BF16),
            jax.ShapeDtypeStruct((copies, 1, cols), F32),
        ],
        scratch_shapes=[pltpu.VMEM((2 * rows, width), BF16)],
        compiler_params=HELD,
        cost_estimate=pl.CostEstimate(
            flops=4 * rows * cols * width,
            bytes_accessed=2 * 2 * rows * cols + 2 * width * cols,
            transcendentals=2 * rows * cols,
        ),
        name="teacher_expo",
    )(place, own, other, protos)


def student_kernel(
    place, own, other, protos, mixed, total_part, dirs, unit, own_v, other_v, store, dirs_v, unit_v, sums, in_sems, out_sems
):
    half = store.shape[1]
    pair = [
        pltpu.make_async_copy(own, own_v, in_sems.at[0]),
        pltpu.make_async_copy(other, other_v, in_sems.at[1]),
    ]
    incoming, outgoing = [], []
    for j in range(half // BLOCK):
        there = pl.ds(pl.multiple_of(place[0] * half + j * BLOCK, BLOCK), BLOCK)
        here = pl.ds(j * BLOCK, BLOCK)
        incoming.append(
            pltpu.make_async_copy(protos.at[:, there], store.at[:, here], in_sems.at[2 + j])
        )
        outgoing.append(
            pltpu.make_async_copy(dirs_v.at[:, here], dirs.at[:, here], out_sems.at[1 + j])
        )
    for copy in pair + incoming:
        copy.start()
    for copy in pair:
        copy.wait()
    unit_v[...] = pair_rows(place[0], own_v[...], other_v[...])
    unit_out = pltpu.make_async_copy(unit_v, unit, out_sems.at[0])
    unit_out.start()
    for j in range(half // BLOCK):
        here = slice(j * BLOCK, (j + 1) * BLOCK)
        incoming[j].wait()
        directions, _ = unit_cols(store[:, here].astype(F32))
        dirs_v[:, here] = directions
        outgoing[j].start()
        values = jnp.exp2(dot(unit_v[...], directions) * student_rate)
        part = fold_lanes(values)
        product = dot_rows(values.astype(BF16), directions)
        sums[...] = part if j == 0 else sums[...] + part
        mixed[...] = product if j == 0 else mixed[...] + product
    total_part[...] = row_to_lanes(sums[...])
    for copy in [unit_out] + outgoing:
        copy.wait()


def student_call(place, own, other, protos):
    rows, width = own.shape
    cols = protos.shape[1] // 2
    return pl.pallas_call(
        student_kernel,
        in_specs=[SMEM, HBM, HBM, HBM],
        out_specs=[VMEM, VMEM, HBM, HBM],
        out_shape=[
            jax.ShapeDtypeStruct((2 * rows, width), F32),
            jax.ShapeDtypeStruct((1, 2 * rows), F32),
            jax.ShapeDtypeStruct((width, cols), BF16),
            jax.ShapeDtypeStruct((2 * rows, width), BF16),
        ],
        scratch_shapes=[
            pltpu.VMEM((rows, width), F32),
            pltpu.VMEM((rows, width), F32),
            pltpu.VMEM((width, cols), BF16),
            pltpu.VMEM((width, cols), BF16),
            pltpu.VMEM((2 * rows, width), BF16),
            pltpu.VMEM((2 * rows, LANES), F32),
            pltpu.SemaphoreType.DMA((2 + cols // BLOCK,)),
            pltpu.SemaphoreType.DMA((1 + cols // BLOCK,)),
        ],
        compiler_params=PARAMS,
        cost_estimate=pl.CostEstimate(
            flops=8 * rows * cols * width,
            bytes_accessed=4 * width * cols + 8 * rows * width,
            transcendentals=2 * rows * cols,
        ),
        name="student_totals",
    )(place, own, other, protos)


def row_slices(expo):
    return [slice(first, first + LANES) for first in range(0, expo.shape[0], LANES)]


class Stream:
    def __init__(self, expo, scratch):
        self.rows = row_slices(expo)
        self.values, self.copies = expo, []
        if scratch:
            self.values, sems = scratch
            for i, here in enumerate(self.rows):
                copy = pltpu.make_async_copy(expo.at[here, :], self.values.at[here, :], sems.at[i])
                copy.start()
                self.copies.append(copy)

    def __iter__(self):
        for i, here in enumerate(self.rows):
            if self.copies:
                self.copies[i].wait()
            yield here


def stream_scratch(expo, held):
    if held:
        return []
    return [pltpu.VMEM(expo.shape, BF16), pltpu.SemaphoreType.DMA((expo.shape[0] // LANES,))]


def scaled_row_sums(values, here, scale):
    total = jnp.zeros((LANES, LANES), F32)
    for at in range(0, values.shape[1], LANES):
        wide = jnp.concatenate([scale[:, at : at + LANES]] * (LANES // 8), axis=0)
        total = total + values[here, at : at + LANES].astype(F32) * wide
    return row_to_lanes(total)


def row_sweep_kernel(proto_total, extra, col_parts, expo, *rest):
    row_part, scale = rest[extra], rest[extra + 1]
    stream = Stream(expo, rest[extra + 2 :])
    copies = row_part.shape[0]
    sums = jnp.sum(col_parts[...], axis=0)
    scale[...] = jnp.broadcast_to(1.0 / (proto_total * sums), scale.shape)
    if extra:
        row_part[:, 1:2, :] = tall(rest[0][...], copies)
    for here in stream:
        row_part[:, 0:1, here] = tall(scaled_row_sums(stream.values, here, scale), copies)


def row_sweep(proto_total, col_parts, expo, copies, held, extra=()):
    rows, cols = expo.shape
    kinds = 1 + len(extra)
    return pl.pallas_call(
        lambda *refs: row_sweep_kernel(proto_total, len(extra), *refs),
        in_specs=[VMEM, VMEM if held else HBM] + [VMEM] * len(extra),
        out_specs=VMEM,
        out_shape=jax.ShapeDtypeStruct((copies, kinds, rows), F32),
        scratch_shapes=[pltpu.VMEM((8, cols), F32)] + stream_scratch(expo, held),
        compiler_params=HELD if held else PARAMS,
        cost_estimate=pl.CostEstimate(
            flops=2 * rows * cols, bytes_accessed=2 * rows * cols, transcendentals=0
        ),
        name="row_sweep",
    )(col_parts, expo, *extra)


def col_sweep_kernel(batch_total, row_parts, expo, col_part, scale, *scratch):
    stream = Stream(expo, scratch)
    copies = col_part.shape[0]
    cols = expo.shape[1]
    sums = jnp.sum(row_parts[...], axis=0)
    scale[...] = lanes_to_rows(1.0 / (batch_total * sums[0:1]))
    if sums.shape[0] > 1:
        col_part[:, :, cols:] = tall(sums[1:2], copies)
    if stream.copies:
        total = [jnp.zeros((8, LANES), F32)] * (cols // LANES)
        for here in stream:
            for j in range(cols // LANES):
                block = stream.values[here, j * LANES : (j + 1) * LANES].astype(F32) * scale[here, :]
                total[j] = total[j] + jnp.sum(block.reshape(LANES // 8, 8, LANES), axis=0)
        for j, part in enumerate(total):
            part = jnp.sum(part, axis=0, keepdims=True)
            col_part[:, :, j * LANES : (j + 1) * LANES] = tall(part, copies)
    else:
        for at in range(0, cols, LANES):
            block = expo[:, at : at + LANES].astype(F32) * scale[...]
            col_part[:, :, at : at + LANES] = tall(jnp.sum(block, axis=0, keepdims=True), copies)


def col_sweep(batch_total, row_parts, expo, copies, held):
    rows, cols = expo.shape
    extra = row_parts.shape[1] - 1
    return pl.pallas_call(
        lambda *refs: col_sweep_kernel(batch_total, *refs),
        in_specs=[VMEM, VMEM if held else HBM],
        out_specs=VMEM,
        out_shape=jax.ShapeDtypeStruct((copies, 1, cols + extra * rows), F32),
        scratch_shapes=[pltpu.VMEM((rows, LANES), F32)] + stream_scratch(expo, held),
        compiler_params=HELD if held else PARAMS,
        cost_estimate=pl.CostEstimate(
            flops=2 * rows * cols, bytes_accessed=2 * rows * cols, transcendentals=0
        ),
        name="col_sweep",
    )(row_parts, expo)


def last_sweep_kernel(
    proto_total, place, col_parts, expo, dirs, unit, student, row_part, own, other, scale, scaled
):
    rows, cols = expo.shape
    width = dirs.shape[0]
    copies = row_part.shape[0]
    half = rows // 2
    wide = 1.0 / (proto_total * jnp.sum(col_parts[:, :, :cols], axis=0))
    scale[...] = jnp.broadcast_to(wide, scale.shape)
    scaled[...] = (dirs[...].astype(F32) * wide).astype(BF16)
    second = place[0] == 1
    products = []
    for first in range(0, rows, half):
        here = slice(first, first + half)
        product = dot_rows(expo[here, :], scaled[...])
        products.append(product)
        meet = fold_lanes(product * unit[here, :].astype(F32))
        row_part[:, 1:2, here] = tall(row_to_lanes(meet), copies)
    for here in row_slices(expo):
        row_part[:, 0:1, here] = tall(scaled_row_sums(expo, here, scale), copies)
    own[:, :width] = jnp.where(second, student[half:, :], student[:half, :])
    other[:, :width] = jnp.where(second, student[:half, :], student[half:, :])
    own[:, width:] = jnp.where(second, products[1], products[0])
    other[:, width:] = jnp.where(second, products[0], products[1])


def last_sweep(proto_total, place, col_parts, expo, dirs, unit, student, copies):
    rows, cols = expo.shape
    width = dirs.shape[0]
    half = (rows // 2, 2 * width)
    return pl.pallas_call(
        lambda *refs: last_sweep_kernel(proto_total, *refs),
        in_specs=[SMEM] + [VMEM] * 5,
        out_specs=[VMEM] * 4,
        out_shape=[
            jax.ShapeDtypeStruct((copies, 2, rows), F32),
            jax.ShapeDtypeStruct(half, F32),
            jax.ShapeDtypeStruct(half, F32),
            jax.ShapeDtypeStruct((8, cols), F32),
        ],
        scratch_shapes=[pltpu.VMEM((width, cols), BF16)],
        compiler_params=HELD,
        cost_estimate=pl.CostEstimate(
            flops=2 * rows * cols * (width + 1),
            bytes_accessed=2 * rows * cols + 2 * width * cols,
            transcendentals=0,
        ),
        name="last_sweep",
    )(place, col_parts, expo, dirs, unit, student)


def wide_kernel(
    place, both, totals, t_protos, s_protos, after, expo, turned, dirs, inverse, mixed, t_dirs
):
    @pl.when(pl.program_id(0) == 0)
    def _():
        t_dirs[...] = unit_cols(t_protos[...].astype(F32))[0]
        dirs[...], norms = unit_cols(s_protos[...].astype(F32))
        inverse[...] = 1.0 / norms
        mixed[...] = jnp.zeros_like(mixed)

    width, cols = dirs.shape
    teacher = both[:, :width].astype(BF16)
    student = both[:, width:].astype(BF16)
    across = student.T
    turned[...] = across
    log_total = lanes_to_rows(jnp.log2(totals[0]))
    shift = jnp.concatenate([log_total] * (BLOCK // LANES), axis=1)
    for first in range(0, cols, BLOCK):
        here = slice(first, first + BLOCK)
        expo[:, here] = jnp.exp2(dot(teacher, t_dirs[:, here]) * teacher_rate).astype(BF16)
        chance = jnp.exp2(dot(student, dirs[:, here]) * student_rate - shift).astype(BF16)
        mixed[:, here] += dot(across, chance)


def wide_call(place, gathered, col_parts, t_protos, s_protos, after, shares, blocks):
    crops, double = gathered.shape
    width = double // 2
    rows = crops // blocks
    cols = t_protos.shape[1] // shares
    last = col_parts.shape[2] // rows - 1
    return pl.pallas_call(
        wide_kernel,
        grid_spec=pltpu.PrefetchScalarGridSpec(
            num_scalar_prefetch=1,
            grid=(blocks,),
            in_specs=[
                pl.BlockSpec((rows, double), lambda i, place: (i, 0)),
                pl.BlockSpec((1, 1, rows), lambda i, place: (2 * i + place[4], 0, last)),
                pl.BlockSpec((width, cols), lambda i, place: (0, place[2])),
                pl.BlockSpec((width, cols), lambda i, place: (0, place[2])),
                whole(TOKEN),
            ],
            out_specs=[
                pl.BlockSpec((rows, cols), lambda i, place: (i, 0)),
                pl.BlockSpec((width, rows), lambda i, place: (0, i)),
                whole((width, cols)),
                whole((1, cols)),
                whole((width, cols)),
            ],
            scratch_shapes=[pltpu.VMEM((width, cols), BF16)],
        ),
        out_shape=[
            jax.ShapeDtypeStruct((crops, cols), BF16),
            jax.ShapeDtypeStruct((width, crops), BF16),
            jax.ShapeDtypeStruct((width, cols), BF16),
            jax.ShapeDtypeStruct((1, cols), F32),
            jax.ShapeDtypeStruct((width, cols), F32),
        ],
        compiler_params=PARAMS,
        cost_estimate=pl.CostEstimate(
            flops=6 * crops * cols * width,
            bytes_accessed=4 * crops * double + 2 * crops * cols,
            transcendentals=2 * crops * cols,
        ),
        name="wide_products",
    )(place, gathered, col_parts, t_protos, s_protos, after)


def finish_kernel(
    place, row_parts, totals, turned, expo, scale, far_scale, dirs, inverse, mixed, grad, loss, *scratch
):
    across, store, total, dirs_v, mixed_v, sems = scratch
    rows = totals.shape[2]
    copies = []
    late = [
        pltpu.make_async_copy(dirs, dirs_v, sems.at[0, across.shape[1] // BLOCK]),
        pltpu.make_async_copy(mixed, mixed_v, sems.at[1, across.shape[1] // BLOCK]),
    ]
    for i in range(totals.shape[0] // 2):
        for first in range(i * rows, (i + 1) * rows, BLOCK):
            here = slice(first, first + BLOCK)
            k = first // BLOCK
            copies.append(
                (
                    here,
                    pltpu.make_async_copy(turned.at[:, here], across.at[:, here], sems.at[0, k]),
                    pltpu.make_async_copy(expo.at[here, :], store.at[here, :], sems.at[1, k]),
                )
            )
    for _, one, two in copies:
        one.start()
        two.start()
    for copy in late:
        copy.start()
    sources = row_parts.shape[0] // (totals.shape[0] // 2)
    terms = jnp.zeros((1, rows), F32)
    done = 0
    for i in range(totals.shape[0] // 2):
        sums = jnp.sum(row_parts[i * sources : (i + 1) * sources], axis=0)
        reciprocal = 1.0 / sums[0:1]
        meet = sums[1:2] * reciprocal * (1.0 / student_temp)
        terms = terms + jnp.log(totals[2 * i + place[4]]) - meet
        for first in range(0, rows, BLOCK):
            here, one, two = copies[done]
            one.wait()
            two.wait()
            factor = reciprocal[:, first : first + BLOCK]
            weighted = (across[:, here].astype(F32) * factor).astype(BF16)
            product = dot(weighted, store[here, :])
            total[...] = product if done == 0 else total[...] + product
            done += 1
    for copy in late:
        copy.wait()
    factor = jnp.where(place[6] == 1, scale[0:1], far_scale[0:1])
    values = mixed_v[...] - factor * total[...]
    wide = dirs_v[...].astype(F32)
    dots = jnp.sum(values * wide, axis=0, keepdims=True)
    values = (values - wide * dots) * (inverse[...] * (1.0 / student_temp))
    grad[...] = values.reshape(grad.shape)
    loss[...] = jnp.broadcast_to(jnp.sum(terms, axis=1, keepdims=True), loss.shape)


def finish_call(
    place, row_parts, col_parts, turned, expo, scale, far_scale, dirs, inverse, mixed, pieces
):
    crops, cols = expo.shape
    width = dirs.shape[0]
    chips = col_parts.shape[0]
    rows = 2 * crops // chips
    last = col_parts.shape[2] // rows - 1
    out = (pieces, width // pieces, cols)
    return pl.pallas_call(
        finish_kernel,
        grid_spec=pltpu.PrefetchScalarGridSpec(
            num_scalar_prefetch=1,
            grid=(1,),
            in_specs=[
                whole(row_parts.shape),
                pl.BlockSpec((chips, 1, rows), lambda i, place: (0, 0, last)),
                HBM,
                HBM,
                pl.BlockSpec((8, cols), lambda i, place: (0, place[3])),
                pl.BlockSpec((8, cols), lambda i, place: (0, place[3])),
                HBM,
                whole((1, cols)),
                HBM,
            ],
            out_specs=[whole(out), whole((1, LANES))],
            scratch_shapes=[
                pltpu.VMEM((width, crops), BF16),
                pltpu.VMEM((crops, cols), BF16),
                pltpu.VMEM((width, cols), F32),
                pltpu.VMEM((width, cols), BF16),
                pltpu.VMEM((width, cols), F32),
                pltpu.SemaphoreType.DMA((2, 1 + crops // BLOCK)),
            ],
        ),
        out_shape=[
            jax.ShapeDtypeStruct(out, F32),
            jax.ShapeDtypeStruct((1, LANES), F32),
        ],
        compiler_params=PARAMS,
        cost_estimate=pl.CostEstimate(
            flops=2 * crops * cols * width,
            bytes_accessed=2 * crops * width + 2 * crops * cols,
            transcendentals=0,
        ),
        name="finish_protos",
    )(place, row_parts, col_parts, turned, expo, scale, far_scale, dirs, inverse, mixed)


COL_AXES = ("x", "zl")
ROW_AXES = ("c", "zh", "y")
CROP_AXES = ("x", "zl", "c")
GATHER_AXES = ("x", "c")
LAST_AXES = ("x", "c", "zh", "y")
SWAP = [(0, 1), (1, 0)]


def exchange(values, axes):
    return lax.all_to_all(values, axes, 0, 0, tiled=True)


def swap(values, axis):
    return lax.ppermute(values, axis, SWAP)


def pick(values, index):
    return lax.dynamic_index_in_dim(values, index, 0, keepdims=False)


def sum_scatter(values):
    near, along = lax.axis_index("zh"), lax.axis_index("y")
    count = values.shape[1]
    half = pick(values, near) + swap(pick(values, 1 - near), "zh")
    total = pick(half, along)
    for step in range(1, count):
        ring = [(i, (i + step) % count) for i in range(count)]
        total = total + lax.ppermute(pick(half, (along + step) % count), "y", ring)
    return total


def on_device(teacher_emb, student_emb, teacher_protos, student_protos):
    core = lax.axis_index("c")
    chip = lax.axis_index(COL_AXES)
    group = lax.axis_index(("zh", "y"))
    chips = lax.axis_size(COL_AXES)
    groups = lax.axis_size(("zh", "y"))
    row_copies = 2 * groups
    shares = lax.axis_size(GATHER_AXES)
    blocks = lax.axis_size("x")
    crops, width = teacher_emb.shape
    batch_total = crops * chips * 2
    proto_total = teacher_protos.shape[1] * groups
    share = lax.axis_index(GATHER_AXES)

    teacher_unit, student_unit, both, place = unit_call(teacher_emb, student_emb)
    teacher_other = swap(teacher_unit, "c")
    gathered = lax.all_gather(both, GATHER_AXES, axis=0, tiled=True)
    student_other = swap(student_unit, "c")
    half = teacher_protos.shape[1] // 2
    half_protos = lax.dynamic_slice_in_dim(teacher_protos, core * half, half, 1)

    expo, col_part = teacher_call(place, teacher_unit, teacher_other, half_protos, chips)
    student_mixed, total_part, dirs, unit = student_call(
        place, student_unit, student_other, student_protos
    )

    col_parts = exchange(col_part, COL_AXES)
    row_part = row_sweep(proto_total, col_parts, expo, row_copies, True)
    row_parts = exchange(row_part, ROW_AXES)
    col_part = col_sweep(batch_total, row_parts, expo, chips, True)
    col_parts = exchange(col_part, COL_AXES)
    row_part = row_sweep(proto_total, col_parts, expo, row_copies, True, (total_part,))
    row_parts = exchange(row_part, ROW_AXES)
    col_part = col_sweep(batch_total, row_parts, expo, chips, True)
    col_parts = exchange(col_part, COL_AXES)
    row_part, own_part, other_part, scale = last_sweep(
        proto_total, place, col_parts, expo, dirs, unit, student_mixed, blocks * row_copies
    )
    row_parts = exchange(row_part, LAST_AXES)
    wide_expo, turned, wide_dirs, inverse, wide_mixed = wide_call(
        place, gathered, col_parts, teacher_protos, student_protos, scale, shares, blocks
    )
    far_scale = swap(scale, "c")

    grad_rows, terms = finish_call(
        place, row_parts, col_parts, turned, wide_expo, scale, far_scale, wide_dirs, inverse,
        wide_mixed, 2 * chips,
    )
    loss = (terms + swap(terms, "zl"))[0, 0] / batch_total
    grad_rows = exchange(grad_rows, CROP_AXES)
    own_rows, cols = grad_rows.shape[1:]
    grad_rows = grad_rows.reshape(blocks, 2, 2, own_rows, cols)
    grad_rows = grad_rows[:, 0] + grad_rows[:, 1]
    grad_prototypes = jnp.moveaxis(grad_rows, 2, 0).reshape(own_rows, shares * cols)

    rows = crops // groups
    far_part, wide_mixed = lax.optimization_barrier((swap(other_part, "c"), wide_mixed))
    summed = sum_scatter(
        (own_part + far_part).reshape(
            lax.axis_size("zh"), lax.axis_size("y"), rows, 2 * width
        )
    )
    first = core * crops + group * rows
    sources = lax.dynamic_slice(
        row_parts, (lax.axis_index("x") * row_copies, 0, first), (row_copies, 1, rows)
    )
    row_sum = jnp.sum(sources, axis=(0, 1))
    total = lax.dynamic_slice(
        col_parts, (chip, 0, col_parts.shape[2] - 2 * crops + first), (1, 1, rows)
    ).reshape(rows)
    grad_unit = summed[:, :width] / total[:, None] - summed[:, width:] / row_sum[:, None]
    grad_unit = grad_unit / student_temp
    own_emb = lax.dynamic_slice_in_dim(student_emb, group * rows, rows, 0)
    s_unit, s_norm = unit_rows(own_emb.astype(F32))
    along = jnp.sum(s_unit * grad_unit, axis=1, keepdims=True)
    grad_embeddings = (grad_unit - s_unit * along) / s_norm
    return (grad_embeddings, grad_prototypes, loss)


def solution(mesh):
    fine = Mesh(mesh.devices.reshape(4, 2, 2, 2, 4), ("x", "zl", "c", "zh", "y"))
    crops, protos = ("x", "zl", "c"), ("zh", "y")
    return jax.shard_map(
        on_device,
        mesh=fine,
        in_specs=(P(crops, None), P(crops, None), P(None, protos), P(None, protos)),
        out_specs=(P(crops + protos, None), P(crops, protos), P()),
        check_vma=False,
    )
```

```python
import math

import jax
import jax.numpy as jnp
from jax import lax
from jax.experimental import pallas as pl
from jax.experimental.pallas import tpu as pltpu
from jax.sharding import Mesh
from jax.sharding import PartitionSpec as P

teacher_temp = 0.07
student_temp = 0.1
norm_eps = 1e-06
log2_e = math.log2(math.e)
teacher_rate = log2_e / teacher_temp
student_rate = log2_e / student_temp

BF16 = jnp.bfloat16
F32 = jnp.float32
LANES = 128
BLOCK = 512
MIB = 1 << 20


PARAMS = pltpu.CompilerParams(vmem_limit_bytes=61 * MIB)
HELD = pltpu.CompilerParams(vmem_limit_bytes=20 * MIB)
TIGHT = pltpu.CompilerParams(vmem_limit_bytes=48 * MIB)


def unit_rows(wide):
    norms = jnp.sqrt(jnp.sum(wide * wide, axis=1, keepdims=True) + norm_eps)
    return wide * (1.0 / norms), norms


def unit_cols(wide):
    norms = jnp.sqrt(jnp.sum(wide * wide, axis=0, keepdims=True) + norm_eps)
    return (wide * (1.0 / norms)).astype(BF16), norms


def dot_rows(left, right):
    return lax.dot_general(left, right, (((1,), (1,)), ((), ())), preferred_element_type=F32)


def dot_cols(left, right):
    return lax.dot_general(left, right, (((0,), (0,)), ((), ())), preferred_element_type=F32)


def dot(left, right):
    return jnp.dot(left, right, preferred_element_type=F32)


def fold_lanes(values):
    total = values[:, :LANES]
    for first in range(LANES, values.shape[1], LANES):
        total = total + values[:, first : first + LANES]
    return total


def row_to_lanes(values):
    return jnp.sum(values.T, axis=0, keepdims=True)


def lanes_to_rows(values):
    return jnp.broadcast_to(values, (LANES, values.shape[1])).T


VMEM = pl.BlockSpec(memory_space=pltpu.VMEM)
SMEM = pl.BlockSpec(memory_space=pltpu.SMEM)
HBM = pl.BlockSpec(memory_space=pltpu.HBM)


def whole(shape):
    return pl.BlockSpec(shape, lambda *_: (0,) * len(shape))


def tall(values, copies):
    return jnp.broadcast_to(values[None], (copies,) + values.shape)


def unit_kernel(teacher, student, teacher_unit, student_unit, both, place):
    width = teacher.shape[1]
    first = unit_rows(teacher[...].astype(F32))[0].astype(BF16).astype(F32)
    second = unit_rows(student[...].astype(F32))[0].astype(BF16).astype(F32)
    teacher_unit[...] = first
    student_unit[...] = second
    both[:, :width] = first
    both[:, width:] = second
    core, x, near, far = (lax.axis_index(axis) for axis in ("c", "x", "zl", "zh"))
    share = 2 * x + core
    here = (share // 4 == core).astype(jnp.int32)
    for i, value in enumerate((core, 2 * x + near, share, share % 4, near, x, here, far)):
        place[i] = value.astype(jnp.int32)


def unit_call(teacher, student):
    rows, width = teacher.shape
    return pl.pallas_call(
        unit_kernel,
        grid=(1,),
        in_specs=[whole((rows, width))] * 2,
        out_specs=[whole((rows, width))] * 2 + [whole((rows, 2 * width)), SMEM],
        out_shape=[
            jax.ShapeDtypeStruct((rows, width), F32),
            jax.ShapeDtypeStruct((rows, width), F32),
            jax.ShapeDtypeStruct((rows, 2 * width), F32),
            jax.ShapeDtypeStruct((8,), jnp.int32),
        ],
        compiler_params=HELD,
        name="unit_rows",
    )(teacher, student)


def pair_rows(core, own, other):
    swap = core == 1
    first = jnp.where(swap, other, own).astype(BF16)
    second = jnp.where(swap, own, other).astype(BF16)
    return jnp.concatenate([first, second], axis=0)


def teacher_kernel(place, own, other, protos, expo, col_part, unit):
    unit[...] = pair_rows(place[0], own[...], other[...])
    for first in range(0, protos.shape[1], BLOCK):
        here = slice(first, first + BLOCK)
        directions, _ = unit_cols(protos[:, here].astype(F32))
        values = jnp.exp2(dot(unit[...], directions) * teacher_rate)
        expo[:, here] = values.astype(BF16)
        col_part[:, here] = jnp.sum(values, axis=0, keepdims=True)


def teacher_call(place, own, other, protos):
    rows, width = own.shape
    cols = protos.shape[1]
    return pl.pallas_call(
        teacher_kernel,
        in_specs=[SMEM, VMEM, VMEM, VMEM],
        out_specs=[VMEM, VMEM],
        out_shape=[
            jax.ShapeDtypeStruct((2 * rows, cols), BF16),
            jax.ShapeDtypeStruct((1, cols), F32),
        ],
        scratch_shapes=[pltpu.VMEM((2 * rows, width), BF16)],
        compiler_params=HELD,
        cost_estimate=pl.CostEstimate(
            flops=4 * rows * cols * width,
            bytes_accessed=2 * 2 * rows * cols + 2 * width * cols,
            transcendentals=2 * rows * cols,
        ),
        name="teacher_expo",
    )(place, own, other, protos)


def add_kernel(one, two, out):
    out[...] = one[...] + two[...]


def add_call(one, two):
    return pl.pallas_call(
        add_kernel,
        in_specs=[VMEM] * 2,
        out_specs=VMEM,
        out_shape=jax.ShapeDtypeStruct(one.shape, F32),
        compiler_params=HELD,
        name="add_parts",
    )(one, two)


def student_kernel(part, place, one, two, sums_in, protos, mixed, sums, dirs, unit, store, sems):
    cols = dirs.shape[1]
    copies = []
    for j in range(cols // BLOCK):
        first = (2 * place[0] + part) * cols + j * BLOCK
        there = pl.ds(pl.multiple_of(first, BLOCK), BLOCK)
        here = pl.ds(j * BLOCK, BLOCK)
        copies.append(pltpu.make_async_copy(protos.at[:, there], store.at[:, here], sems.at[j]))
    for copy in copies:
        copy.start()
    if part == 0:
        unit[...] = pair_rows(place[0], one[...], two[...])
        mixed[...] = jnp.zeros_like(mixed)
    else:
        unit[...] = one[...]
        mixed[...] = two[...]
    total = sums_in[...]
    for j, copy in enumerate(copies):
        here = slice(j * BLOCK, (j + 1) * BLOCK)
        copy.wait()
        directions, _ = unit_cols(store[:, here].astype(F32))
        dirs[:, here] = directions
        values = jnp.exp2(dot(unit[...], directions) * student_rate)
        total = total + row_to_lanes(fold_lanes(values))
        mixed[...] += dot_rows(values.astype(BF16), directions)
    sums[...] = total


def student_call(part, place, one, two, sums, protos):
    width = protos.shape[0]
    rows = sums.shape[1]
    cols = protos.shape[1] // 4
    return pl.pallas_call(
        lambda *refs: student_kernel(part, *refs),
        in_specs=[SMEM, VMEM, VMEM, VMEM, HBM],
        out_specs=[VMEM] * 4,
        out_shape=[
            jax.ShapeDtypeStruct((rows, width), F32),
            jax.ShapeDtypeStruct((1, rows), F32),
            jax.ShapeDtypeStruct((width, cols), BF16),
            jax.ShapeDtypeStruct((rows, width), BF16),
        ],
        scratch_shapes=[
            pltpu.VMEM((width, cols), BF16),
            pltpu.SemaphoreType.DMA((cols // BLOCK,)),
        ],
        compiler_params=TIGHT,
        cost_estimate=pl.CostEstimate(
            flops=4 * rows * cols * width,
            bytes_accessed=4 * width * cols + 8 * rows * width,
            transcendentals=rows * cols,
        ),
        name="student_totals",
    )(place, one, two, sums, protos)


def row_slices(expo):
    return [slice(first, first + LANES) for first in range(0, expo.shape[0], LANES)]


def scaled_row_sums(values, here, scale):
    total = jnp.zeros((LANES, LANES), F32)
    for at in range(0, values.shape[1], LANES):
        wide = jnp.concatenate([scale[:, at : at + LANES]] * (LANES // 8), axis=0)
        total = total + values[here, at : at + LANES].astype(F32) * wide
    return row_to_lanes(total)


def row_sweep_kernel(proto_total, extra, expo, *rest):
    parts, (row_part, scale) = rest[extra:-2], rest[-2:]
    copies = row_part.shape[0]
    sums = 0.0
    for part in parts:
        sums = sums + (jnp.sum(part[...], axis=0) if len(part.shape) == 3 else part[...])
    scale[...] = jnp.broadcast_to(1.0 / (proto_total * sums), scale.shape)
    if extra:
        row_part[:, 1:2, :] = tall(rest[0][...], copies)
    for here in row_slices(expo):
        row_part[:, 0:1, here] = tall(scaled_row_sums(expo, here, scale), copies)


def row_sweep(proto_total, parts, expo, copies, extra=()):
    rows, cols = expo.shape
    kinds = 1 + len(extra)
    return pl.pallas_call(
        lambda *refs: row_sweep_kernel(proto_total, len(extra), *refs),
        in_specs=[VMEM] * (1 + len(extra) + len(parts)),
        out_specs=VMEM,
        out_shape=jax.ShapeDtypeStruct((copies, kinds, rows), F32),
        scratch_shapes=[pltpu.VMEM((8, cols), F32)],
        compiler_params=HELD,
        cost_estimate=pl.CostEstimate(
            flops=2 * rows * cols, bytes_accessed=2 * rows * cols, transcendentals=0
        ),
        name="row_sweep",
    )(expo, *extra, *parts)


def col_sweep_kernel(batch_total, row_parts, expo, col_part, scale):
    copies = col_part.shape[0]
    cols = expo.shape[1]
    sums = jnp.sum(row_parts[...], axis=0)
    scale[...] = lanes_to_rows(1.0 / (batch_total * sums[0:1]))
    if sums.shape[0] > 1:
        col_part[:, :, cols:] = tall(sums[1:2], copies)
    for at in range(0, cols, LANES):
        block = expo[:, at : at + LANES].astype(F32) * scale[...]
        col_part[:, :, at : at + LANES] = tall(jnp.sum(block, axis=0, keepdims=True), copies)


def col_sweep(batch_total, row_parts, expo, copies):
    rows, cols = expo.shape
    extra = rows * (row_parts.shape[1] - 1)
    return pl.pallas_call(
        lambda *refs: col_sweep_kernel(batch_total, *refs),
        in_specs=[VMEM] * 2,
        out_specs=VMEM,
        out_shape=jax.ShapeDtypeStruct((copies, 1, cols + extra), F32),
        scratch_shapes=[pltpu.VMEM((rows, LANES), F32)],
        compiler_params=HELD,
        cost_estimate=pl.CostEstimate(
            flops=2 * rows * cols, bytes_accessed=2 * rows * cols, transcendentals=0
        ),
        name="col_sweep",
    )(row_parts, expo)


def last_sweep_kernel(
    proto_total, place, col_parts, expo, dirs, far_dirs, unit, student, row_part, own, other,
    scale_out, scale, scaled,
):
    rows, cols = expo.shape
    width = dirs.shape[0]
    copies = row_part.shape[0]
    half, quarter = rows // 2, rows // 4
    wide = 1.0 / (proto_total * jnp.sum(col_parts[:, :, :cols], axis=0))
    scale_out[...] = wide
    scale[...] = jnp.broadcast_to(wide, scale.shape)
    part = dirs.shape[1]
    scaled[:, :part] = (dirs[...].astype(F32) * wide[:, :part]).astype(BF16)
    scaled[:, part:] = (far_dirs[...].astype(F32) * wide[:, part:]).astype(BF16)
    products = []
    for first in range(0, rows, half):
        here = slice(first, first + half)
        product = dot_rows(expo[here, :], scaled[...])
        products.append(product)
        meet = fold_lanes(product * unit[here, :].astype(F32))
        row_part[:, 1:2, here] = tall(row_to_lanes(meet), copies)
    for here in row_slices(expo):
        row_part[:, 0:1, here] = tall(scaled_row_sums(expo, here, scale), copies)
    core, far = place[0] == 1, place[7] == 1

    def choose(where, one, two):
        return jnp.where(where, two, one), jnp.where(where, one, two)

    for at, kind in ((0, [student[:half, :], student[half:, :]]), (width, products)):
        for out, values in zip((own, other), choose(core, *kind)):
            stay, go = choose(far, values[:quarter], values[quarter:])
            out[0, :, at : at + width] = stay
            out[1, :, at : at + width] = go


def last_sweep(proto_total, place, col_parts, expo, dirs, far_dirs, unit, student, copies):
    rows, cols = expo.shape
    width = dirs.shape[0]
    half = (2, rows // 4, 2 * width)
    return pl.pallas_call(
        lambda *refs: last_sweep_kernel(proto_total, *refs),
        in_specs=[SMEM] + [VMEM] * 6,
        out_specs=[VMEM] * 4,
        out_shape=[
            jax.ShapeDtypeStruct((copies, 2, rows), F32),
            jax.ShapeDtypeStruct(half, F32),
            jax.ShapeDtypeStruct(half, F32),
            jax.ShapeDtypeStruct((1, cols), F32),
        ],
        scratch_shapes=[pltpu.VMEM((8, cols), F32), pltpu.VMEM((width, cols), BF16)],
        compiler_params=HELD,
        cost_estimate=pl.CostEstimate(
            flops=2 * rows * cols * (width + 1),
            bytes_accessed=2 * rows * cols + 2 * width * cols,
            transcendentals=0,
        ),
        name="last_sweep",
    )(place, col_parts, expo, dirs, far_dirs, unit, student)


def wide_kernel(
    place, both, totals, t_protos, s_protos, expo, turned, dirs, inverse, mixed, t_dirs
):
    @pl.when(pl.program_id(0) == 0)
    def _():
        t_dirs[...] = unit_cols(t_protos[...].astype(F32))[0]
        dirs[...], norms = unit_cols(s_protos[...].astype(F32))
        inverse[...] = 1.0 / norms
        mixed[...] = jnp.zeros_like(mixed)

    width, cols = dirs.shape
    teacher = both[:, :width].astype(BF16)
    student = both[:, width:].astype(BF16)
    across = student.T
    turned[...] = across
    log_total = lanes_to_rows(jnp.log2(totals[0]))
    shift = jnp.concatenate([log_total] * (BLOCK // LANES), axis=1)
    for first in range(0, cols, BLOCK):
        here = slice(first, first + BLOCK)
        expo[:, here] = jnp.exp2(dot(teacher, t_dirs[:, here]) * teacher_rate).astype(BF16)
        chance = jnp.exp2(dot(student, dirs[:, here]) * student_rate - shift).astype(BF16)
        mixed[:, here] += dot(across, chance)


def wide_call(place, gathered, col_parts, t_protos, s_protos, shares, blocks):
    crops, double = gathered.shape
    width = double // 2
    rows = crops // blocks
    cols = t_protos.shape[1] // shares
    last = col_parts.shape[2] // rows - 1
    return pl.pallas_call(
        wide_kernel,
        grid_spec=pltpu.PrefetchScalarGridSpec(
            num_scalar_prefetch=1,
            grid=(blocks,),
            in_specs=[
                pl.BlockSpec((rows, double), lambda i, place: (i, 0)),
                pl.BlockSpec((1, 1, rows), lambda i, place: (2 * i + place[4], 0, last)),
                pl.BlockSpec((width, cols), lambda i, place: (0, place[2])),
                pl.BlockSpec((width, cols), lambda i, place: (0, place[2])),
            ],
            out_specs=[
                pl.BlockSpec((rows, cols), lambda i, place: (i, 0)),
                pl.BlockSpec((width, rows), lambda i, place: (0, i)),
                whole((width, cols)),
                whole((1, cols)),
                whole((width, cols)),
            ],
            scratch_shapes=[pltpu.VMEM((width, cols), BF16)],
        ),
        out_shape=[
            jax.ShapeDtypeStruct((crops, cols), BF16),
            jax.ShapeDtypeStruct((width, crops), BF16),
            jax.ShapeDtypeStruct((width, cols), BF16),
            jax.ShapeDtypeStruct((1, cols), F32),
            jax.ShapeDtypeStruct((width, cols), F32),
        ],
        compiler_params=PARAMS,
        cost_estimate=pl.CostEstimate(
            flops=6 * crops * cols * width,
            bytes_accessed=4 * crops * double + 2 * crops * cols,
            transcendentals=2 * crops * cols,
        ),
        name="wide_products",
    )(place, gathered, col_parts, t_protos, s_protos)


def finish_kernel(
    place, row_parts, totals, turned, expo, scale, far_scale, dirs, inverse, mixed, grad, loss, *scratch
):
    across, store, total, dirs_v, mixed_v, sems = scratch
    rows = totals.shape[2]
    copies = []
    late = [
        pltpu.make_async_copy(dirs, dirs_v, sems.at[0, across.shape[1] // BLOCK]),
        pltpu.make_async_copy(mixed, mixed_v, sems.at[1, across.shape[1] // BLOCK]),
    ]
    for i in range(totals.shape[0] // 2):
        for first in range(i * rows, (i + 1) * rows, BLOCK):
            here = slice(first, first + BLOCK)
            k = first // BLOCK
            copies.append(
                (
                    here,
                    pltpu.make_async_copy(turned.at[:, here], across.at[:, here], sems.at[0, k]),
                    pltpu.make_async_copy(expo.at[here, :], store.at[here, :], sems.at[1, k]),
                )
            )
    for _, one, two in copies:
        one.start()
        two.start()
    for copy in late:
        copy.start()
    sources = row_parts.shape[0] // (totals.shape[0] // 2)
    terms = jnp.zeros((1, rows), F32)
    done = 0
    for i in range(totals.shape[0] // 2):
        sums = jnp.sum(row_parts[i * sources : (i + 1) * sources], axis=0)
        reciprocal = 1.0 / sums[0:1]
        meet = sums[1:2] * reciprocal * (1.0 / student_temp)
        terms = terms + jnp.log(totals[2 * i + place[4]]) - meet
        for first in range(0, rows, BLOCK):
            here, one, two = copies[done]
            one.wait()
            two.wait()
            factor = reciprocal[:, first : first + BLOCK]
            weighted = (across[:, here].astype(F32) * factor).astype(BF16)
            product = dot(weighted, store[here, :])
            total[...] = product if done == 0 else total[...] + product
            done += 1
    for copy in late:
        copy.wait()
    factor = jnp.where(place[6] == 1, scale[...], far_scale[...])
    values = mixed_v[...] - factor * total[...]
    wide = dirs_v[...].astype(F32)
    dots = jnp.sum(values * wide, axis=0, keepdims=True)
    values = (values - wide * dots) * (inverse[...] * (1.0 / student_temp))
    grad[...] = values.reshape(grad.shape)
    loss[...] = jnp.broadcast_to(jnp.sum(terms, axis=1, keepdims=True), loss.shape)


def finish_call(
    place, row_parts, col_parts, turned, expo, scale, far_scale, dirs, inverse, mixed, pieces
):
    crops, cols = expo.shape
    width = dirs.shape[0]
    chips = col_parts.shape[0]
    rows = 2 * crops // chips
    last = col_parts.shape[2] // rows - 1
    out = (pieces, width // pieces, cols)
    return pl.pallas_call(
        finish_kernel,
        grid_spec=pltpu.PrefetchScalarGridSpec(
            num_scalar_prefetch=1,
            grid=(1,),
            in_specs=[
                whole(row_parts.shape),
                pl.BlockSpec((chips, 1, rows), lambda i, place: (0, 0, last)),
                HBM,
                HBM,
                pl.BlockSpec((1, cols), lambda i, place: (0, place[3])),
                pl.BlockSpec((1, cols), lambda i, place: (0, place[3])),
                HBM,
                whole((1, cols)),
                HBM,
            ],
            out_specs=[whole(out), whole((1, LANES))],
            scratch_shapes=[
                pltpu.VMEM((width, crops), BF16),
                pltpu.VMEM((crops, cols), BF16),
                pltpu.VMEM((width, cols), F32),
                pltpu.VMEM((width, cols), BF16),
                pltpu.VMEM((width, cols), F32),
                pltpu.SemaphoreType.DMA((2, 1 + crops // BLOCK)),
            ],
        ),
        out_shape=[
            jax.ShapeDtypeStruct(out, F32),
            jax.ShapeDtypeStruct((1, LANES), F32),
        ],
        compiler_params=PARAMS,
        cost_estimate=pl.CostEstimate(
            flops=2 * crops * cols * width,
            bytes_accessed=2 * crops * width + 2 * crops * cols,
            transcendentals=0,
        ),
        name="finish_protos",
    )(place, row_parts, col_parts, turned, expo, scale, far_scale, dirs, inverse, mixed)


COL_AXES = ("x", "zl")
ROW_AXES = ("c", "zh", "y")
CROP_AXES = ("x", "zl", "c")
GATHER_AXES = ("x", "c")
LAST_AXES = ("x", "c", "zh", "y")
SWAP = [(0, 1), (1, 0)]


def exchange(values, axes):
    return lax.all_to_all(values, axes, 0, 0, tiled=True)


def swap(values, axis):
    return lax.ppermute(values, axis, SWAP)


def pick(values, index):
    return lax.dynamic_index_in_dim(values, index, 0, keepdims=False)


def sum_scatter(stay, go):
    along = lax.axis_index("y")
    half = stay + swap(go, "zh")
    count = half.shape[0]
    total = pick(half, along)
    for step in range(1, count):
        ring = [(i, (i + step) % count) for i in range(count)]
        total = total + lax.ppermute(pick(half, (along + step) % count), "y", ring)
    return total


def on_device(teacher_emb, student_emb, teacher_protos, student_protos):
    core = lax.axis_index("c")
    chip = lax.axis_index(COL_AXES)
    group = lax.axis_index(("zh", "y"))
    chips = lax.axis_size(COL_AXES)
    groups = lax.axis_size(("zh", "y"))
    row_copies = 2 * groups
    shares = lax.axis_size(GATHER_AXES)
    blocks = lax.axis_size("x")
    crops, width = teacher_emb.shape
    batch_total = crops * chips * 2
    proto_total = teacher_protos.shape[1] * groups
    share = lax.axis_index(GATHER_AXES)

    teacher_unit, student_unit, both, place = unit_call(teacher_emb, student_emb)
    teacher_other = swap(teacher_unit, "c")
    gathered = lax.all_gather(both, GATHER_AXES, axis=0, tiled=True)
    student_other = swap(student_unit, "c")
    half = teacher_protos.shape[1] // 2
    half_protos = lax.dynamic_slice_in_dim(teacher_protos, core * half, half, 1)

    expo, col_part = teacher_call(place, teacher_unit, teacher_other, half_protos)

    near_part = swap(col_part, "zl")
    no_sums = jnp.zeros((1, 2 * crops), F32)
    mixed, sums, dirs, unit = student_call(
        0, place, student_unit, student_other, no_sums, student_protos
    )
    near_part, mixed = lax.optimization_barrier((near_part, mixed))
    col_part = add_call(col_part, near_part)
    col_parts = [
        lax.ppermute(col_part, "x", [(i, (i + step) % blocks) for i in range(blocks)])
        for step in range(1, blocks)
    ]
    student_mixed, total_part, far_dirs, unit = student_call(
        1, place, unit, mixed, sums, student_protos
    )
    col_parts, total_part = lax.optimization_barrier((col_parts, total_part))
    row_part = row_sweep(proto_total, [col_part] + col_parts, expo, row_copies)
    row_parts = exchange(row_part, ROW_AXES)
    col_part = col_sweep(batch_total, row_parts, expo, chips)
    col_parts = exchange(col_part, COL_AXES)
    row_part = row_sweep(proto_total, [col_parts], expo, row_copies, (total_part,))
    row_parts = exchange(row_part, ROW_AXES)
    col_part = col_sweep(batch_total, row_parts, expo, chips)
    col_parts = exchange(col_part, COL_AXES)
    row_part, own_part, other_part, scale = last_sweep(
        proto_total, place, col_parts, expo, dirs, far_dirs, unit, student_mixed,
        blocks * row_copies,
    )
    row_parts = exchange(row_part, LAST_AXES)
    gathered, scale = lax.optimization_barrier((gathered, scale))
    wide_expo, turned, wide_dirs, inverse, wide_mixed = wide_call(
        place, gathered, col_parts, teacher_protos, student_protos, shares, blocks
    )
    far_scale = swap(scale, "c")

    grad_rows, terms = finish_call(
        place, row_parts, col_parts, turned, wide_expo, scale, far_scale, wide_dirs, inverse,
        wide_mixed, 2 * chips,
    )
    loss = (terms + swap(terms, "zl"))[0, 0] / batch_total
    grad_rows = exchange(grad_rows, CROP_AXES)
    own_rows, cols = grad_rows.shape[1:]
    grad_rows = grad_rows.reshape(blocks, 2, 2, own_rows, cols)
    grad_rows = grad_rows[:, 0] + grad_rows[:, 1]
    grad_prototypes = jnp.moveaxis(grad_rows, 2, 0).reshape(own_rows, shares * cols)

    rows = crops // groups
    far_part, wide_mixed = lax.optimization_barrier((swap(other_part, "c"), wide_mixed))
    pieces = (2, lax.axis_size("y"), rows, 2 * width)
    own_part, far_part = own_part.reshape(pieces), far_part.reshape(pieces)
    summed = sum_scatter(own_part[0] + far_part[0], own_part[1] + far_part[1])
    first = core * crops + group * rows
    sources = lax.dynamic_slice(
        row_parts, (lax.axis_index("x") * row_copies, 0, first), (row_copies, 1, rows)
    )
    row_sum = jnp.sum(sources, axis=(0, 1))
    total = lax.dynamic_slice(
        col_parts, (chip, 0, col_parts.shape[2] - 2 * crops + first), (1, 1, rows)
    ).reshape(rows)
    grad_unit = summed[:, :width] / total[:, None] - summed[:, width:] / row_sum[:, None]
    grad_unit = grad_unit / student_temp
    own_emb = lax.dynamic_slice_in_dim(student_emb, group * rows, rows, 0)
    s_unit, s_norm = unit_rows(own_emb.astype(F32))
    along = jnp.sum(s_unit * grad_unit, axis=1, keepdims=True)
    grad_embeddings = (grad_unit - s_unit * along) / s_norm
    return (grad_embeddings, grad_prototypes, loss)


def solution(mesh):
    fine = Mesh(mesh.devices.reshape(4, 2, 2, 2, 4), ("x", "zl", "c", "zh", "y"))
    crops, protos = ("x", "zl", "c"), ("zh", "y")
    return jax.shard_map(
        on_device,
        mesh=fine,
        in_specs=(P(crops, None), P(crops, None), P(None, protos), P(None, protos)),
        out_specs=(P(crops + protos, None), P(crops, protos), P()),
        check_vma=False,
    )
```

```python
import math

import jax
import jax.numpy as jnp
from jax import lax
from jax.experimental import pallas as pl
from jax.experimental.pallas import tpu as pltpu
from jax.sharding import Mesh
from jax.sharding import PartitionSpec as P

teacher_temp = 0.07
student_temp = 0.1
norm_eps = 1e-06
log2_e = math.log2(math.e)
teacher_rate = log2_e / teacher_temp
student_rate = log2_e / student_temp

BF16 = jnp.bfloat16
F32 = jnp.float32
LANES = 128
BLOCK = 512
MIB = 1 << 20


PARAMS = pltpu.CompilerParams(vmem_limit_bytes=61 * MIB)
HELD = pltpu.CompilerParams(vmem_limit_bytes=20 * MIB)
TIGHT = pltpu.CompilerParams(vmem_limit_bytes=48 * MIB)


def unit_rows(wide):
    norms = jnp.sqrt(jnp.sum(wide * wide, axis=1, keepdims=True) + norm_eps)
    return wide * (1.0 / norms), norms


def unit_cols(wide):
    norms = jnp.sqrt(jnp.sum(wide * wide, axis=0, keepdims=True) + norm_eps)
    return (wide * (1.0 / norms)).astype(BF16), norms


def dot_rows(left, right):
    return lax.dot_general(left, right, (((1,), (1,)), ((), ())), preferred_element_type=F32)


def dot_cols(left, right):
    return lax.dot_general(left, right, (((0,), (0,)), ((), ())), preferred_element_type=F32)


def dot(left, right):
    return jnp.dot(left, right, preferred_element_type=F32)


def fold_lanes(values):
    total = values[:, :LANES]
    for first in range(LANES, values.shape[1], LANES):
        total = total + values[:, first : first + LANES]
    return total


def row_to_lanes(values):
    return jnp.sum(values.T, axis=0, keepdims=True)


def lanes_to_rows(values):
    return jnp.broadcast_to(values, (LANES, values.shape[1])).T


VMEM = pl.BlockSpec(memory_space=pltpu.VMEM)
SMEM = pl.BlockSpec(memory_space=pltpu.SMEM)
HBM = pl.BlockSpec(memory_space=pltpu.HBM)


def whole(shape):
    return pl.BlockSpec(shape, lambda *_: (0,) * len(shape))


def tall(values, copies):
    return jnp.broadcast_to(values[None], (copies,) + values.shape)


def unit_kernel(teacher, student, teacher_unit, student_unit, both, place):
    width = teacher.shape[1]
    first = unit_rows(teacher[...].astype(F32))[0].astype(BF16).astype(F32)
    second = unit_rows(student[...].astype(F32))[0].astype(BF16).astype(F32)
    teacher_unit[...] = first
    student_unit[...] = second
    both[:, :width] = first
    both[:, width:] = second
    core, x, near, far = (lax.axis_index(axis) for axis in ("c", "x", "zl", "zh"))
    share = 2 * x + core
    here = (share // 4 == core).astype(jnp.int32)
    for i, value in enumerate((core, 2 * x + near, share, share % 4, near, x, here, far)):
        place[i] = value.astype(jnp.int32)


def unit_call(teacher, student):
    rows, width = teacher.shape
    return pl.pallas_call(
        unit_kernel,
        grid=(1,),
        in_specs=[whole((rows, width))] * 2,
        out_specs=[whole((rows, width))] * 2 + [whole((rows, 2 * width)), SMEM],
        out_shape=[
            jax.ShapeDtypeStruct((rows, width), F32),
            jax.ShapeDtypeStruct((rows, width), F32),
            jax.ShapeDtypeStruct((rows, 2 * width), F32),
            jax.ShapeDtypeStruct((8,), jnp.int32),
        ],
        compiler_params=HELD,
        name="unit_rows",
    )(teacher, student)


def pair_rows(core, own, other):
    swap = core == 1
    first = jnp.where(swap, other, own).astype(BF16)
    second = jnp.where(swap, own, other).astype(BF16)
    return jnp.concatenate([first, second], axis=0)


def teacher_kernel(place, own, other, protos, expo, col_part, unit):
    unit[...] = pair_rows(place[0], own[...], other[...])
    for first in range(0, protos.shape[1], BLOCK):
        here = slice(first, first + BLOCK)
        directions, _ = unit_cols(protos[:, here].astype(F32))
        values = jnp.exp2(dot(unit[...], directions) * teacher_rate)
        expo[:, here] = values.astype(BF16)
        col_part[:, here] = jnp.sum(values, axis=0, keepdims=True)


def teacher_call(place, own, other, protos):
    rows, width = own.shape
    cols = protos.shape[1]
    return pl.pallas_call(
        teacher_kernel,
        in_specs=[SMEM, VMEM, VMEM, VMEM],
        out_specs=[VMEM, VMEM],
        out_shape=[
            jax.ShapeDtypeStruct((2 * rows, cols), BF16),
            jax.ShapeDtypeStruct((1, cols), F32),
        ],
        scratch_shapes=[pltpu.VMEM((2 * rows, width), BF16)],
        compiler_params=HELD,
        cost_estimate=pl.CostEstimate(
            flops=4 * rows * cols * width,
            bytes_accessed=2 * 2 * rows * cols + 2 * width * cols,
            transcendentals=2 * rows * cols,
        ),
        name="teacher_expo",
    )(place, own, other, protos)


def add_kernel(one, two, out):
    out[...] = one[...] + two[...]


def add_call(one, two):
    return pl.pallas_call(
        add_kernel,
        in_specs=[VMEM] * 2,
        out_specs=VMEM,
        out_shape=jax.ShapeDtypeStruct(one.shape, F32),
        compiler_params=HELD,
        name="add_parts",
    )(one, two)


def student_kernel(part, place, one, two, sums_in, protos, mixed, sums, dirs, unit, store, sems):
    cols = dirs.shape[1]
    copies = []
    for j in range(cols // BLOCK):
        first = (2 * place[0] + part) * cols + j * BLOCK
        there = pl.ds(pl.multiple_of(first, BLOCK), BLOCK)
        here = pl.ds(j * BLOCK, BLOCK)
        copies.append(pltpu.make_async_copy(protos.at[:, there], store.at[:, here], sems.at[j]))
    for copy in copies:
        copy.start()
    if part == 0:
        unit[...] = pair_rows(place[0], one[...], two[...])
        mixed[...] = jnp.zeros_like(mixed)
    else:
        unit[...] = one[...]
        mixed[...] = two[...]
    total = sums_in[...]
    for copy in copies:
        copy.wait()
    for j in range(cols // BLOCK):
        here = slice(j * BLOCK, (j + 1) * BLOCK)
        directions, _ = unit_cols(store[:, here].astype(F32))
        dirs[:, here] = directions
        values = jnp.exp2(dot(unit[...], directions) * student_rate)
        total = total + row_to_lanes(fold_lanes(values))
        mixed[...] += dot_rows(values.astype(BF16), directions)
    sums[...] = total


def student_call(part, place, one, two, sums, protos):
    width = protos.shape[0]
    rows = sums.shape[1]
    cols = protos.shape[1] // 4
    return pl.pallas_call(
        lambda *refs: student_kernel(part, *refs),
        in_specs=[SMEM, VMEM, VMEM, VMEM, HBM],
        out_specs=[VMEM] * 4,
        out_shape=[
            jax.ShapeDtypeStruct((rows, width), F32),
            jax.ShapeDtypeStruct((1, rows), F32),
            jax.ShapeDtypeStruct((width, cols), BF16),
            jax.ShapeDtypeStruct((rows, width), BF16),
        ],
        scratch_shapes=[
            pltpu.VMEM((width, cols), BF16),
            pltpu.SemaphoreType.DMA((cols // BLOCK,)),
        ],
        compiler_params=TIGHT,
        cost_estimate=pl.CostEstimate(
            flops=4 * rows * cols * width,
            bytes_accessed=4 * width * cols + 8 * rows * width,
            transcendentals=rows * cols,
        ),
        name="student_totals",
    )(place, one, two, sums, protos)


def row_slices(expo):
    return [slice(first, first + LANES) for first in range(0, expo.shape[0], LANES)]


def scaled_row_sums(values, here, scale):
    total = jnp.zeros((LANES, LANES), F32)
    for at in range(0, values.shape[1], LANES):
        wide = jnp.concatenate([scale[:, at : at + LANES]] * (LANES // 8), axis=0)
        total = total + values[here, at : at + LANES].astype(F32) * wide
    return row_to_lanes(total)


def row_sweep_kernel(proto_total, extra, expo, *rest):
    parts, (row_part, scale) = rest[extra:-2], rest[-2:]
    copies = row_part.shape[0]
    sums = 0.0
    for part in parts:
        sums = sums + (jnp.sum(part[...], axis=0) if len(part.shape) == 3 else part[...])
    scale[...] = jnp.broadcast_to(1.0 / (proto_total * sums), scale.shape)
    if extra:
        row_part[:, 1:2, :] = tall(rest[0][...], copies)
    for here in row_slices(expo):
        row_part[:, 0:1, here] = tall(scaled_row_sums(expo, here, scale), copies)


def row_sweep(proto_total, parts, expo, copies, extra=()):
    rows, cols = expo.shape
    kinds = 1 + len(extra)
    return pl.pallas_call(
        lambda *refs: row_sweep_kernel(proto_total, len(extra), *refs),
        in_specs=[VMEM] * (1 + len(extra) + len(parts)),
        out_specs=VMEM,
        out_shape=jax.ShapeDtypeStruct((copies, kinds, rows), F32),
        scratch_shapes=[pltpu.VMEM((8, cols), F32)],
        compiler_params=HELD,
        cost_estimate=pl.CostEstimate(
            flops=2 * rows * cols, bytes_accessed=2 * rows * cols, transcendentals=0
        ),
        name="row_sweep",
    )(expo, *extra, *parts)


def col_sweep_kernel(batch_total, row_parts, expo, col_part, scale):
    copies = col_part.shape[0]
    cols = expo.shape[1]
    sums = jnp.sum(row_parts[...], axis=0)
    scale[...] = lanes_to_rows(1.0 / (batch_total * sums[0:1]))
    if sums.shape[0] > 1:
        col_part[:, :, cols:] = tall(sums[1:2], copies)
    for at in range(0, cols, LANES):
        block = expo[:, at : at + LANES].astype(F32) * scale[...]
        col_part[:, :, at : at + LANES] = tall(jnp.sum(block, axis=0, keepdims=True), copies)


def col_sweep(batch_total, row_parts, expo, copies):
    rows, cols = expo.shape
    extra = rows * (row_parts.shape[1] - 1)
    return pl.pallas_call(
        lambda *refs: col_sweep_kernel(batch_total, *refs),
        in_specs=[VMEM] * 2,
        out_specs=VMEM,
        out_shape=jax.ShapeDtypeStruct((copies, 1, cols + extra), F32),
        scratch_shapes=[pltpu.VMEM((rows, LANES), F32)],
        compiler_params=HELD,
        cost_estimate=pl.CostEstimate(
            flops=2 * rows * cols, bytes_accessed=2 * rows * cols, transcendentals=0
        ),
        name="col_sweep",
    )(row_parts, expo)


def last_sweep_kernel(
    proto_total, place, col_parts, expo, dirs, far_dirs, unit, student, row_part, own, other,
    scale_out, scale, scaled,
):
    rows, cols = expo.shape
    width = dirs.shape[0]
    copies = row_part.shape[0]
    half, quarter = rows // 2, rows // 4
    wide = 1.0 / (proto_total * jnp.sum(col_parts[:, :, :cols], axis=0))
    scale_out[...] = wide
    scale[...] = jnp.broadcast_to(wide, scale.shape)
    part = dirs.shape[1]
    scaled[:, :part] = (dirs[...].astype(F32) * wide[:, :part]).astype(BF16)
    scaled[:, part:] = (far_dirs[...].astype(F32) * wide[:, part:]).astype(BF16)
    products = []
    for first in range(0, rows, half):
        here = slice(first, first + half)
        product = dot_rows(expo[here, :], scaled[...])
        products.append(product)
        meet = fold_lanes(product * unit[here, :].astype(F32))
        row_part[:, 1:2, here] = tall(row_to_lanes(meet), copies)
    for here in row_slices(expo):
        row_part[:, 0:1, here] = tall(scaled_row_sums(expo, here, scale), copies)
    core, far = place[0] == 1, place[7] == 1

    def choose(where, one, two):
        return jnp.where(where, two, one), jnp.where(where, one, two)

    for at, kind in ((0, [student[:half, :], student[half:, :]]), (width, products)):
        for out, values in zip((own, other), choose(core, *kind)):
            stay, go = choose(far, values[:quarter], values[quarter:])
            out[0, :, at : at + width] = stay
            out[1, :, at : at + width] = go


def last_sweep(proto_total, place, col_parts, expo, dirs, far_dirs, unit, student, copies):
    rows, cols = expo.shape
    width = dirs.shape[0]
    half = (2, rows // 4, 2 * width)
    return pl.pallas_call(
        lambda *refs: last_sweep_kernel(proto_total, *refs),
        in_specs=[SMEM] + [VMEM] * 6,
        out_specs=[VMEM] * 4,
        out_shape=[
            jax.ShapeDtypeStruct((copies, 2, rows), F32),
            jax.ShapeDtypeStruct(half, F32),
            jax.ShapeDtypeStruct(half, F32),
            jax.ShapeDtypeStruct((1, cols), F32),
        ],
        scratch_shapes=[pltpu.VMEM((8, cols), F32), pltpu.VMEM((width, cols), BF16)],
        compiler_params=HELD,
        cost_estimate=pl.CostEstimate(
            flops=2 * rows * cols * (width + 1),
            bytes_accessed=2 * rows * cols + 2 * width * cols,
            transcendentals=0,
        ),
        name="last_sweep",
    )(place, col_parts, expo, dirs, far_dirs, unit, student)


def wide_kernel(
    place, both, totals, t_protos, s_protos, expo, turned, dirs, inverse, mixed, t_dirs
):
    @pl.when(pl.program_id(0) == 0)
    def _():
        t_dirs[...] = unit_cols(t_protos[...].astype(F32))[0]
        dirs[...], norms = unit_cols(s_protos[...].astype(F32))
        inverse[...] = 1.0 / norms
        mixed[...] = jnp.zeros_like(mixed)

    width, cols = dirs.shape
    teacher = both[:, :width].astype(BF16)
    student = both[:, width:].astype(BF16)
    across = student.T
    turned[...] = across
    log_total = lanes_to_rows(jnp.log2(totals[0]))
    shift = jnp.concatenate([log_total] * (BLOCK // LANES), axis=1)
    for first in range(0, cols, BLOCK):
        here = slice(first, first + BLOCK)
        expo[:, here] = jnp.exp2(dot(teacher, t_dirs[:, here]) * teacher_rate).astype(BF16)
        chance = jnp.exp2(dot(student, dirs[:, here]) * student_rate - shift).astype(BF16)
        mixed[:, here] += dot(across, chance)


def wide_call(place, gathered, col_parts, t_protos, s_protos, shares, blocks):
    crops, double = gathered.shape
    width = double // 2
    rows = crops // blocks
    cols = t_protos.shape[1] // shares
    last = col_parts.shape[2] // rows - 1
    return pl.pallas_call(
        wide_kernel,
        grid_spec=pltpu.PrefetchScalarGridSpec(
            num_scalar_prefetch=1,
            grid=(blocks,),
            in_specs=[
                pl.BlockSpec((rows, double), lambda i, place: (i, 0)),
                pl.BlockSpec((1, 1, rows), lambda i, place: (2 * i + place[4], 0, last)),
                pl.BlockSpec((width, cols), lambda i, place: (0, place[2])),
                pl.BlockSpec((width, cols), lambda i, place: (0, place[2])),
            ],
            out_specs=[
                pl.BlockSpec((rows, cols), lambda i, place: (i, 0)),
                pl.BlockSpec((width, rows), lambda i, place: (0, i)),
                whole((width, cols)),
                whole((1, cols)),
                whole((width, cols)),
            ],
            scratch_shapes=[pltpu.VMEM((width, cols), BF16)],
        ),
        out_shape=[
            jax.ShapeDtypeStruct((crops, cols), BF16),
            jax.ShapeDtypeStruct((width, crops), BF16),
            jax.ShapeDtypeStruct((width, cols), BF16),
            jax.ShapeDtypeStruct((1, cols), F32),
            jax.ShapeDtypeStruct((width, cols), F32),
        ],
        compiler_params=PARAMS,
        cost_estimate=pl.CostEstimate(
            flops=6 * crops * cols * width,
            bytes_accessed=4 * crops * double + 2 * crops * cols,
            transcendentals=2 * crops * cols,
        ),
        name="wide_products",
    )(place, gathered, col_parts, t_protos, s_protos)


def finish_kernel(
    place, row_parts, totals, turned, expo, scale, far_scale, dirs, inverse, mixed, grad, loss, *scratch
):
    across, store, total, dirs_v, mixed_v, sems = scratch
    rows = totals.shape[2]
    copies = []
    late = [
        pltpu.make_async_copy(dirs, dirs_v, sems.at[0, across.shape[1] // BLOCK]),
        pltpu.make_async_copy(mixed, mixed_v, sems.at[1, across.shape[1] // BLOCK]),
    ]
    for i in range(totals.shape[0] // 2):
        for first in range(i * rows, (i + 1) * rows, BLOCK):
            here = slice(first, first + BLOCK)
            k = first // BLOCK
            copies.append(
                (
                    here,
                    pltpu.make_async_copy(turned.at[:, here], across.at[:, here], sems.at[0, k]),
                    pltpu.make_async_copy(expo.at[here, :], store.at[here, :], sems.at[1, k]),
                )
            )
    for _, one, two in copies:
        one.start()
        two.start()
    for copy in late:
        copy.start()
    sources = row_parts.shape[0] // (totals.shape[0] // 2)
    terms = jnp.zeros((1, rows), F32)
    done = 0
    for i in range(totals.shape[0] // 2):
        sums = jnp.sum(row_parts[i * sources : (i + 1) * sources], axis=0)
        reciprocal = 1.0 / sums[0:1]
        meet = sums[1:2] * reciprocal * (1.0 / student_temp)
        terms = terms + jnp.log(totals[2 * i + place[4]]) - meet
        for first in range(0, rows, BLOCK):
            here, one, two = copies[done]
            one.wait()
            two.wait()
            factor = reciprocal[:, first : first + BLOCK]
            weighted = (across[:, here].astype(F32) * factor).astype(BF16)
            product = dot(weighted, store[here, :])
            total[...] = product if done == 0 else total[...] + product
            done += 1
    for copy in late:
        copy.wait()
    factor = jnp.where(place[6] == 1, scale[...], far_scale[...])
    values = mixed_v[...] - factor * total[...]
    wide = dirs_v[...].astype(F32)
    dots = jnp.sum(values * wide, axis=0, keepdims=True)
    values = (values - wide * dots) * (inverse[...] * (1.0 / student_temp))
    grad[...] = values.reshape(grad.shape)
    loss[...] = jnp.broadcast_to(jnp.sum(terms, axis=1, keepdims=True), loss.shape)


def finish_call(
    place, row_parts, col_parts, turned, expo, scale, far_scale, dirs, inverse, mixed, pieces
):
    crops, cols = expo.shape
    width = dirs.shape[0]
    chips = col_parts.shape[0]
    rows = 2 * crops // chips
    last = col_parts.shape[2] // rows - 1
    out = (pieces, width // pieces, cols)
    return pl.pallas_call(
        finish_kernel,
        grid_spec=pltpu.PrefetchScalarGridSpec(
            num_scalar_prefetch=1,
            grid=(1,),
            in_specs=[
                whole(row_parts.shape),
                pl.BlockSpec((chips, 1, rows), lambda i, place: (0, 0, last)),
                HBM,
                HBM,
                pl.BlockSpec((1, cols), lambda i, place: (0, place[3])),
                pl.BlockSpec((1, cols), lambda i, place: (0, place[3])),
                HBM,
                whole((1, cols)),
                HBM,
            ],
            out_specs=[whole(out), whole((1, LANES))],
            scratch_shapes=[
                pltpu.VMEM((width, crops), BF16),
                pltpu.VMEM((crops, cols), BF16),
                pltpu.VMEM((width, cols), F32),
                pltpu.VMEM((width, cols), BF16),
                pltpu.VMEM((width, cols), F32),
                pltpu.SemaphoreType.DMA((2, 1 + crops // BLOCK)),
            ],
        ),
        out_shape=[
            jax.ShapeDtypeStruct(out, F32),
            jax.ShapeDtypeStruct((1, LANES), F32),
        ],
        compiler_params=PARAMS,
        cost_estimate=pl.CostEstimate(
            flops=2 * crops * cols * width,
            bytes_accessed=2 * crops * width + 2 * crops * cols,
            transcendentals=0,
        ),
        name="finish_protos",
    )(place, row_parts, col_parts, turned, expo, scale, far_scale, dirs, inverse, mixed)


def join_kernel(pieces, out):
    count, rows, cols = pieces.shape
    for share in range(count // 2):
        first = 4 * (share // 2) + share % 2
        out[:, share * cols : (share + 1) * cols] = pieces[first] + pieces[first + 2]


def join_call(pieces):
    count, rows, cols = pieces.shape
    return pl.pallas_call(
        join_kernel,
        in_specs=[VMEM],
        out_specs=VMEM,
        out_shape=jax.ShapeDtypeStruct((rows, count // 2 * cols), F32),
        compiler_params=HELD,
        name="join_pieces",
    )(pieces)


COL_AXES = ("x", "zl")
ROW_AXES = ("c", "zh", "y")
CROP_AXES = ("x", "zl", "c")
GATHER_AXES = ("x", "c")
LAST_AXES = ("x", "c", "zh", "y")
SWAP = [(0, 1), (1, 0)]


def exchange(values, axes):
    return lax.all_to_all(values, axes, 0, 0, tiled=True)


def swap(values, axis):
    return lax.ppermute(values, axis, SWAP)


def pick(values, index):
    return lax.dynamic_index_in_dim(values, index, 0, keepdims=False)


def sum_scatter(stay, go):
    along = lax.axis_index("y")
    half = stay + swap(go, "zh")
    count = half.shape[0]
    total = pick(half, along)
    for step in range(1, count):
        ring = [(i, (i + step) % count) for i in range(count)]
        total = total + lax.ppermute(pick(half, (along + step) % count), "y", ring)
    return total


def on_device(teacher_emb, student_emb, teacher_protos, student_protos):
    core = lax.axis_index("c")
    chip = lax.axis_index(COL_AXES)
    group = lax.axis_index(("zh", "y"))
    chips = lax.axis_size(COL_AXES)
    groups = lax.axis_size(("zh", "y"))
    row_copies = 2 * groups
    shares = lax.axis_size(GATHER_AXES)
    blocks = lax.axis_size("x")
    crops, width = teacher_emb.shape
    batch_total = crops * chips * 2
    proto_total = teacher_protos.shape[1] * groups
    share = lax.axis_index(GATHER_AXES)

    teacher_unit, student_unit, both, place = unit_call(teacher_emb, student_emb)
    teacher_other = swap(teacher_unit, "c")
    gathered = lax.all_gather(both, GATHER_AXES, axis=0, tiled=True)
    student_other = swap(student_unit, "c")
    half = teacher_protos.shape[1] // 2
    half_protos = lax.dynamic_slice_in_dim(teacher_protos, core * half, half, 1)

    expo, col_part = teacher_call(place, teacher_unit, teacher_other, half_protos)

    near_part = swap(col_part, "zl")
    no_sums = jnp.zeros((1, 2 * crops), F32)
    mixed, sums, dirs, unit = student_call(
        0, place, student_unit, student_other, no_sums, student_protos
    )
    near_part, mixed = lax.optimization_barrier((near_part, mixed))
    col_part = add_call(col_part, near_part)
    col_parts = [
        lax.ppermute(col_part, "x", [(i, (i + step) % blocks) for i in range(blocks)])
        for step in range(1, blocks)
    ]
    student_mixed, total_part, far_dirs, unit = student_call(
        1, place, unit, mixed, sums, student_protos
    )
    col_parts, total_part = lax.optimization_barrier((col_parts, total_part))
    row_part = row_sweep(proto_total, [col_part] + col_parts, expo, row_copies)
    row_parts = exchange(row_part, ROW_AXES)
    col_part = col_sweep(batch_total, row_parts, expo, chips)
    col_parts = exchange(col_part, COL_AXES)
    row_part = row_sweep(proto_total, [col_parts], expo, row_copies, (total_part,))
    row_parts = exchange(row_part, ROW_AXES)
    col_part = col_sweep(batch_total, row_parts, expo, chips)
    col_parts = exchange(col_part, COL_AXES)
    row_part, own_part, other_part, scale = last_sweep(
        proto_total, place, col_parts, expo, dirs, far_dirs, unit, student_mixed,
        blocks * row_copies,
    )
    row_parts = exchange(row_part, LAST_AXES)
    gathered, scale = lax.optimization_barrier((gathered, scale))
    wide_expo, turned, wide_dirs, inverse, wide_mixed = wide_call(
        place, gathered, col_parts, teacher_protos, student_protos, shares, blocks
    )
    far_scale = swap(scale, "c")

    grad_rows, terms = finish_call(
        place, row_parts, col_parts, turned, wide_expo, scale, far_scale, wide_dirs, inverse,
        wide_mixed, 2 * chips,
    )
    loss = (terms + swap(terms, "zl"))[0, 0] / batch_total
    grad_rows = exchange(grad_rows, CROP_AXES)
    grad_prototypes = join_call(grad_rows)

    rows = crops // groups
    far_part, wide_mixed = lax.optimization_barrier((swap(other_part, "c"), wide_mixed))
    pieces = (2, lax.axis_size("y"), rows, 2 * width)
    own_part, far_part = own_part.reshape(pieces), far_part.reshape(pieces)
    summed = sum_scatter(own_part[0] + far_part[0], own_part[1] + far_part[1])
    first = core * crops + group * rows
    sources = lax.dynamic_slice(
        row_parts, (lax.axis_index("x") * row_copies, 0, first), (row_copies, 1, rows)
    )
    row_sum = jnp.sum(sources, axis=(0, 1))
    total = lax.dynamic_slice(
        col_parts, (chip, 0, col_parts.shape[2] - 2 * crops + first), (1, 1, rows)
    ).reshape(rows)
    grad_unit = summed[:, :width] / total[:, None] - summed[:, width:] / row_sum[:, None]
    grad_unit = grad_unit / student_temp
    own_emb = lax.dynamic_slice_in_dim(student_emb, group * rows, rows, 0)
    s_unit, s_norm = unit_rows(own_emb.astype(F32))
    along = jnp.sum(s_unit * grad_unit, axis=1, keepdims=True)
    grad_embeddings = (grad_unit - s_unit * along) / s_norm
    return (grad_embeddings, grad_prototypes, loss)


def solution(mesh):
    fine = Mesh(mesh.devices.reshape(4, 2, 2, 2, 4), ("x", "zl", "c", "zh", "y"))
    crops, protos = ("x", "zl", "c"), ("zh", "y")
    return jax.shard_map(
        on_device,
        mesh=fine,
        in_specs=(P(crops, None), P(crops, None), P(None, protos), P(None, protos)),
        out_specs=(P(crops + protos, None), P(crops, protos), P()),
        check_vma=False,
    )
```

```python
import math

import jax
import jax.numpy as jnp
from jax import lax
from jax.experimental import pallas as pl
from jax.experimental.pallas import tpu as pltpu
from jax.sharding import Mesh
from jax.sharding import PartitionSpec as P

teacher_temp = 0.07
student_temp = 0.1
norm_eps = 1e-06
log2_e = math.log2(math.e)
teacher_rate = log2_e / teacher_temp
student_rate = log2_e / student_temp

BF16 = jnp.bfloat16
F32 = jnp.float32
LANES = 128
BLOCK = 512
MIB = 1 << 20


PARAMS = pltpu.CompilerParams(vmem_limit_bytes=61 * MIB)
HELD = pltpu.CompilerParams(vmem_limit_bytes=20 * MIB)
TIGHT = pltpu.CompilerParams(vmem_limit_bytes=48 * MIB)


def unit_rows(wide):
    norms = jnp.sqrt(jnp.sum(wide * wide, axis=1, keepdims=True) + norm_eps)
    return wide * (1.0 / norms), norms


def unit_cols(wide):
    norms = jnp.sqrt(jnp.sum(wide * wide, axis=0, keepdims=True) + norm_eps)
    return (wide * (1.0 / norms)).astype(BF16), norms


def dot_rows(left, right):
    return lax.dot_general(left, right, (((1,), (1,)), ((), ())), preferred_element_type=F32)


def dot_cols(left, right):
    return lax.dot_general(left, right, (((0,), (0,)), ((), ())), preferred_element_type=F32)


def dot(left, right):
    return jnp.dot(left, right, preferred_element_type=F32)


def fold_lanes(values):
    total = values[:, :LANES]
    for first in range(LANES, values.shape[1], LANES):
        total = total + values[:, first : first + LANES]
    return total


def row_to_lanes(values):
    return jnp.sum(values.T, axis=0, keepdims=True)


def lanes_to_rows(values):
    return jnp.broadcast_to(values, (LANES, values.shape[1])).T


VMEM = pl.BlockSpec(memory_space=pltpu.VMEM)
SMEM = pl.BlockSpec(memory_space=pltpu.SMEM)
HBM = pl.BlockSpec(memory_space=pltpu.HBM)


def whole(shape):
    return pl.BlockSpec(shape, lambda *_: (0,) * len(shape))


def tall(values, copies):
    return jnp.broadcast_to(values[None], (copies,) + values.shape)


def unit_kernel(teacher, student, teacher_unit, student_unit, both, place):
    width = teacher.shape[1]
    first = unit_rows(teacher[...].astype(F32))[0].astype(BF16).astype(F32)
    second = unit_rows(student[...].astype(F32))[0].astype(BF16).astype(F32)
    teacher_unit[...] = first
    student_unit[...] = second
    both[:, :width] = first
    both[:, width:] = second
    core, x, near, far = (lax.axis_index(axis) for axis in ("c", "x", "zl", "zh"))
    share = 2 * x + core
    here = (share // 4 == core).astype(jnp.int32)
    for i, value in enumerate((core, 2 * x + near, share, share % 4, near, x, here, far)):
        place[i] = value.astype(jnp.int32)


def unit_call(teacher, student):
    rows, width = teacher.shape
    return pl.pallas_call(
        unit_kernel,
        grid=(1,),
        in_specs=[whole((rows, width))] * 2,
        out_specs=[whole((rows, width))] * 2 + [whole((rows, 2 * width)), SMEM],
        out_shape=[
            jax.ShapeDtypeStruct((rows, width), F32),
            jax.ShapeDtypeStruct((rows, width), F32),
            jax.ShapeDtypeStruct((rows, 2 * width), F32),
            jax.ShapeDtypeStruct((8,), jnp.int32),
        ],
        compiler_params=HELD,
        name="unit_rows",
    )(teacher, student)


def pair_rows(core, own, other):
    swap = core == 1
    first = jnp.where(swap, other, own).astype(BF16)
    second = jnp.where(swap, own, other).astype(BF16)
    return jnp.concatenate([first, second], axis=0)


def teacher_kernel(place, own, other, protos, expo, col_part, unit, store, sem):
    half = store.shape[1]
    there = pl.ds(pl.multiple_of(place[0] * half, half), half)
    copy = pltpu.make_async_copy(protos.at[:, there], store, sem)
    copy.start()
    unit[...] = pair_rows(place[0], own[...], other[...])
    copy.wait()
    for first in range(0, half, BLOCK):
        here = slice(first, first + BLOCK)
        directions, _ = unit_cols(store[:, here].astype(F32))
        values = jnp.exp2(dot(unit[...], directions) * teacher_rate)
        expo[:, here] = values.astype(BF16)
        col_part[:, here] = jnp.sum(values, axis=0, keepdims=True)


def teacher_call(place, own, other, protos):
    rows, width = own.shape
    cols = protos.shape[1] // 2
    return pl.pallas_call(
        teacher_kernel,
        in_specs=[SMEM, VMEM, VMEM, HBM],
        out_specs=[VMEM, VMEM],
        out_shape=[
            jax.ShapeDtypeStruct((2 * rows, cols), BF16),
            jax.ShapeDtypeStruct((1, cols), F32),
        ],
        scratch_shapes=[
            pltpu.VMEM((2 * rows, width), BF16),
            pltpu.VMEM((width, cols), BF16),
            pltpu.SemaphoreType.DMA,
        ],
        compiler_params=TIGHT,
        cost_estimate=pl.CostEstimate(
            flops=4 * rows * cols * width,
            bytes_accessed=2 * 2 * rows * cols + 2 * width * cols,
            transcendentals=2 * rows * cols,
        ),
        name="teacher_expo",
    )(place, own, other, protos)


def add_kernel(one, two, out):
    out[...] = one[...] + two[...]


def add_call(one, two):
    return pl.pallas_call(
        add_kernel,
        in_specs=[VMEM] * 2,
        out_specs=VMEM,
        out_shape=jax.ShapeDtypeStruct(one.shape, F32),
        compiler_params=HELD,
        name="add_parts",
    )(one, two)


def student_kernel(part, place, one, two, sums_in, protos, mixed, sums, dirs, unit, store, sems):
    cols = dirs.shape[1]
    copies = []
    for j in range(cols // BLOCK):
        first = (2 * place[0] + part) * cols + j * BLOCK
        there = pl.ds(pl.multiple_of(first, BLOCK), BLOCK)
        here = pl.ds(j * BLOCK, BLOCK)
        copies.append(pltpu.make_async_copy(protos.at[:, there], store.at[:, here], sems.at[j]))
    for copy in copies:
        copy.start()
    if part == 0:
        unit[...] = pair_rows(place[0], one[...], two[...])
        mixed[...] = jnp.zeros_like(mixed)
    else:
        unit[...] = one[...]
        mixed[...] = two[...]
    total = sums_in[...]
    for copy in copies:
        copy.wait()
    for j in range(cols // BLOCK):
        here = slice(j * BLOCK, (j + 1) * BLOCK)
        directions, _ = unit_cols(store[:, here].astype(F32))
        dirs[:, here] = directions
        values = jnp.exp2(dot(unit[...], directions) * student_rate)
        total = total + row_to_lanes(fold_lanes(values))
        mixed[...] += dot_rows(values.astype(BF16), directions)
    sums[...] = total


def student_call(part, place, one, two, sums, protos):
    width = protos.shape[0]
    rows = sums.shape[1]
    cols = protos.shape[1] // 4
    return pl.pallas_call(
        lambda *refs: student_kernel(part, *refs),
        in_specs=[SMEM, VMEM, VMEM, VMEM, HBM],
        out_specs=[VMEM] * 4,
        out_shape=[
            jax.ShapeDtypeStruct((rows, width), F32),
            jax.ShapeDtypeStruct((1, rows), F32),
            jax.ShapeDtypeStruct((width, cols), BF16),
            jax.ShapeDtypeStruct((rows, width), BF16),
        ],
        scratch_shapes=[
            pltpu.VMEM((width, cols), BF16),
            pltpu.SemaphoreType.DMA((cols // BLOCK,)),
        ],
        compiler_params=TIGHT,
        cost_estimate=pl.CostEstimate(
            flops=4 * rows * cols * width,
            bytes_accessed=4 * width * cols + 8 * rows * width,
            transcendentals=rows * cols,
        ),
        name="student_totals",
    )(place, one, two, sums, protos)


def row_slices(expo):
    return [slice(first, first + LANES) for first in range(0, expo.shape[0], LANES)]


def scaled_row_sums(values, here, scale):
    total = jnp.zeros((LANES, LANES), F32)
    for at in range(0, values.shape[1], LANES):
        wide = jnp.concatenate([scale[:, at : at + LANES]] * (LANES // 8), axis=0)
        total = total + values[here, at : at + LANES].astype(F32) * wide
    return row_to_lanes(total)


def row_sweep_kernel(proto_total, extra, expo, *rest):
    parts, (row_part, scale) = rest[extra:-2], rest[-2:]
    copies = row_part.shape[0]
    sums = 0.0
    for part in parts:
        sums = sums + (jnp.sum(part[...], axis=0) if len(part.shape) == 3 else part[...])
    scale[...] = jnp.broadcast_to(1.0 / (proto_total * sums), scale.shape)
    if extra:
        row_part[:, 1:2, :] = tall(rest[0][...], copies)
    for here in row_slices(expo):
        row_part[:, 0:1, here] = tall(scaled_row_sums(expo, here, scale), copies)


def row_sweep(proto_total, parts, expo, copies, extra=()):
    rows, cols = expo.shape
    kinds = 1 + len(extra)
    return pl.pallas_call(
        lambda *refs: row_sweep_kernel(proto_total, len(extra), *refs),
        in_specs=[VMEM] * (1 + len(extra) + len(parts)),
        out_specs=VMEM,
        out_shape=jax.ShapeDtypeStruct((copies, kinds, rows), F32),
        scratch_shapes=[pltpu.VMEM((8, cols), F32)],
        compiler_params=HELD,
        cost_estimate=pl.CostEstimate(
            flops=2 * rows * cols, bytes_accessed=2 * rows * cols, transcendentals=0
        ),
        name="row_sweep",
    )(expo, *extra, *parts)


def col_sweep_kernel(batch_total, row_parts, expo, col_part, scale):
    copies = col_part.shape[0]
    cols = expo.shape[1]
    sums = jnp.sum(row_parts[...], axis=0)
    scale[...] = lanes_to_rows(1.0 / (batch_total * sums[0:1]))
    if sums.shape[0] > 1:
        col_part[:, :, cols:] = tall(sums[1:2], copies)
    for at in range(0, cols, LANES):
        block = expo[:, at : at + LANES].astype(F32) * scale[...]
        col_part[:, :, at : at + LANES] = tall(jnp.sum(block, axis=0, keepdims=True), copies)


def col_sweep(batch_total, row_parts, expo, copies):
    rows, cols = expo.shape
    extra = rows * (row_parts.shape[1] - 1)
    return pl.pallas_call(
        lambda *refs: col_sweep_kernel(batch_total, *refs),
        in_specs=[VMEM] * 2,
        out_specs=VMEM,
        out_shape=jax.ShapeDtypeStruct((copies, 1, cols + extra), F32),
        scratch_shapes=[pltpu.VMEM((rows, LANES), F32)],
        compiler_params=HELD,
        cost_estimate=pl.CostEstimate(
            flops=2 * rows * cols, bytes_accessed=2 * rows * cols, transcendentals=0
        ),
        name="col_sweep",
    )(row_parts, expo)


def last_sweep_kernel(
    proto_total, place, col_parts, expo, dirs, far_dirs, unit, student, row_part, own, other,
    scale_out, scale, scaled,
):
    rows, cols = expo.shape
    width = dirs.shape[0]
    copies = row_part.shape[0]
    half, quarter = rows // 2, rows // 4
    wide = 1.0 / (proto_total * jnp.sum(col_parts[:, :, :cols], axis=0))
    scale_out[...] = wide
    scale[...] = jnp.broadcast_to(wide, scale.shape)
    part = dirs.shape[1]
    scaled[:, :part] = (dirs[...].astype(F32) * wide[:, :part]).astype(BF16)
    scaled[:, part:] = (far_dirs[...].astype(F32) * wide[:, part:]).astype(BF16)
    products = []
    for first in range(0, rows, half):
        here = slice(first, first + half)
        product = dot_rows(expo[here, :], scaled[...])
        products.append(product)
        meet = fold_lanes(product * unit[here, :].astype(F32))
        row_part[:, 1:2, here] = tall(row_to_lanes(meet), copies)
    for here in row_slices(expo):
        row_part[:, 0:1, here] = tall(scaled_row_sums(expo, here, scale), copies)
    core, far = place[0] == 1, place[7] == 1

    def choose(where, one, two):
        return jnp.where(where, two, one), jnp.where(where, one, two)

    for at, kind in ((0, [student[:half, :], student[half:, :]]), (width, products)):
        for out, values in zip((own, other), choose(core, *kind)):
            stay, go = choose(far, values[:quarter], values[quarter:])
            out[0, :, at : at + width] = stay
            out[1, :, at : at + width] = go


def last_sweep(proto_total, place, col_parts, expo, dirs, far_dirs, unit, student, copies):
    rows, cols = expo.shape
    width = dirs.shape[0]
    half = (2, rows // 4, 2 * width)
    return pl.pallas_call(
        lambda *refs: last_sweep_kernel(proto_total, *refs),
        in_specs=[SMEM] + [VMEM] * 6,
        out_specs=[VMEM] * 4,
        out_shape=[
            jax.ShapeDtypeStruct((copies, 2, rows), F32),
            jax.ShapeDtypeStruct(half, F32),
            jax.ShapeDtypeStruct(half, F32),
            jax.ShapeDtypeStruct((1, cols), F32),
        ],
        scratch_shapes=[pltpu.VMEM((8, cols), F32), pltpu.VMEM((width, cols), BF16)],
        compiler_params=HELD,
        cost_estimate=pl.CostEstimate(
            flops=2 * rows * cols * (width + 1),
            bytes_accessed=2 * rows * cols + 2 * width * cols,
            transcendentals=0,
        ),
        name="last_sweep",
    )(place, col_parts, expo, dirs, far_dirs, unit, student)


def wide_kernel(
    place, both, totals, t_protos, s_protos, expo, turned, dirs, inverse, mixed, t_dirs
):
    @pl.when(pl.program_id(0) == 0)
    def _():
        t_dirs[...] = unit_cols(t_protos[...].astype(F32))[0]
        dirs[...], norms = unit_cols(s_protos[...].astype(F32))
        inverse[...] = 1.0 / norms
        mixed[...] = jnp.zeros_like(mixed)

    width, cols = dirs.shape
    teacher = both[:, :width].astype(BF16)
    student = both[:, width:].astype(BF16)
    across = student.T
    turned[...] = across
    log_total = lanes_to_rows(jnp.log2(totals[0]))
    shift = jnp.concatenate([log_total] * (BLOCK // LANES), axis=1)
    for first in range(0, cols, BLOCK):
        here = slice(first, first + BLOCK)
        expo[:, here] = jnp.exp2(dot(teacher, t_dirs[:, here]) * teacher_rate).astype(BF16)
        chance = jnp.exp2(dot(student, dirs[:, here]) * student_rate - shift).astype(BF16)
        mixed[:, here] += dot(across, chance)


def wide_call(place, gathered, col_parts, t_protos, s_protos, shares, blocks):
    crops, double = gathered.shape
    width = double // 2
    rows = crops // blocks
    cols = t_protos.shape[1] // shares
    last = col_parts.shape[2] // rows - 1
    return pl.pallas_call(
        wide_kernel,
        grid_spec=pltpu.PrefetchScalarGridSpec(
            num_scalar_prefetch=1,
            grid=(blocks,),
            in_specs=[
                pl.BlockSpec((rows, double), lambda i, place: (i, 0)),
                pl.BlockSpec((1, 1, rows), lambda i, place: (2 * i + place[4], 0, last)),
                pl.BlockSpec((width, cols), lambda i, place: (0, place[2])),
                pl.BlockSpec((width, cols), lambda i, place: (0, place[2])),
            ],
            out_specs=[
                pl.BlockSpec((rows, cols), lambda i, place: (i, 0)),
                pl.BlockSpec((width, rows), lambda i, place: (0, i)),
                whole((width, cols)),
                whole((1, cols)),
                whole((width, cols)),
            ],
            scratch_shapes=[pltpu.VMEM((width, cols), BF16)],
        ),
        out_shape=[
            jax.ShapeDtypeStruct((crops, cols), BF16),
            jax.ShapeDtypeStruct((width, crops), BF16),
            jax.ShapeDtypeStruct((width, cols), BF16),
            jax.ShapeDtypeStruct((1, cols), F32),
            jax.ShapeDtypeStruct((width, cols), F32),
        ],
        compiler_params=PARAMS,
        cost_estimate=pl.CostEstimate(
            flops=6 * crops * cols * width,
            bytes_accessed=4 * crops * double + 2 * crops * cols,
            transcendentals=2 * crops * cols,
        ),
        name="wide_products",
    )(place, gathered, col_parts, t_protos, s_protos)


def finish_kernel(
    place, row_parts, totals, turned, expo, scale, far_scale, dirs, inverse, mixed, grad, loss, *scratch
):
    across, store, total, dirs_v, mixed_v, sems = scratch
    rows = totals.shape[2]
    copies = []
    late = [
        pltpu.make_async_copy(dirs, dirs_v, sems.at[0, across.shape[1] // BLOCK]),
        pltpu.make_async_copy(mixed, mixed_v, sems.at[1, across.shape[1] // BLOCK]),
    ]
    for i in range(totals.shape[0] // 2):
        for first in range(i * rows, (i + 1) * rows, BLOCK):
            here = slice(first, first + BLOCK)
            k = first // BLOCK
            copies.append(
                (
                    here,
                    pltpu.make_async_copy(turned.at[:, here], across.at[:, here], sems.at[0, k]),
                    pltpu.make_async_copy(expo.at[here, :], store.at[here, :], sems.at[1, k]),
                )
            )
    for _, one, two in copies:
        one.start()
        two.start()
    for copy in late:
        copy.start()
    sources = row_parts.shape[0] // (totals.shape[0] // 2)
    terms = jnp.zeros((1, rows), F32)
    done = 0
    for i in range(totals.shape[0] // 2):
        sums = jnp.sum(row_parts[i * sources : (i + 1) * sources], axis=0)
        reciprocal = 1.0 / sums[0:1]
        meet = sums[1:2] * reciprocal * (1.0 / student_temp)
        terms = terms + jnp.log(totals[2 * i + place[4]]) - meet
        for first in range(0, rows, BLOCK):
            here, one, two = copies[done]
            one.wait()
            two.wait()
            factor = reciprocal[:, first : first + BLOCK]
            weighted = (across[:, here].astype(F32) * factor).astype(BF16)
            product = dot(weighted, store[here, :])
            total[...] = product if done == 0 else total[...] + product
            done += 1
    for copy in late:
        copy.wait()
    factor = jnp.where(place[6] == 1, scale[...], far_scale[...])
    values = mixed_v[...] - factor * total[...]
    wide = dirs_v[...].astype(F32)
    dots = jnp.sum(values * wide, axis=0, keepdims=True)
    values = (values - wide * dots) * (inverse[...] * (1.0 / student_temp))
    grad[...] = values.reshape(grad.shape)
    loss[...] = jnp.broadcast_to(jnp.sum(terms, axis=1, keepdims=True), loss.shape)


def finish_call(
    place, row_parts, col_parts, turned, expo, scale, far_scale, dirs, inverse, mixed, pieces
):
    crops, cols = expo.shape
    width = dirs.shape[0]
    chips = col_parts.shape[0]
    rows = 2 * crops // chips
    last = col_parts.shape[2] // rows - 1
    out = (pieces, width // pieces, cols)
    return pl.pallas_call(
        finish_kernel,
        grid_spec=pltpu.PrefetchScalarGridSpec(
            num_scalar_prefetch=1,
            grid=(1,),
            in_specs=[
                whole(row_parts.shape),
                pl.BlockSpec((chips, 1, rows), lambda i, place: (0, 0, last)),
                HBM,
                HBM,
                pl.BlockSpec((1, cols), lambda i, place: (0, place[3])),
                pl.BlockSpec((1, cols), lambda i, place: (0, place[3])),
                HBM,
                whole((1, cols)),
                HBM,
            ],
            out_specs=[whole(out), whole((1, LANES))],
            scratch_shapes=[
                pltpu.VMEM((width, crops), BF16),
                pltpu.VMEM((crops, cols), BF16),
                pltpu.VMEM((width, cols), F32),
                pltpu.VMEM((width, cols), BF16),
                pltpu.VMEM((width, cols), F32),
                pltpu.SemaphoreType.DMA((2, 1 + crops // BLOCK)),
            ],
        ),
        out_shape=[
            jax.ShapeDtypeStruct(out, F32),
            jax.ShapeDtypeStruct((1, LANES), F32),
        ],
        compiler_params=PARAMS,
        cost_estimate=pl.CostEstimate(
            flops=2 * crops * cols * width,
            bytes_accessed=2 * crops * width + 2 * crops * cols,
            transcendentals=0,
        ),
        name="finish_protos",
    )(place, row_parts, col_parts, turned, expo, scale, far_scale, dirs, inverse, mixed)


def join_kernel(pieces, out):
    count, rows, cols = pieces.shape
    for share in range(count // 2):
        first = 4 * (share // 2) + share % 2
        out[:, share * cols : (share + 1) * cols] = pieces[first] + pieces[first + 2]


def join_call(pieces):
    count, rows, cols = pieces.shape
    return pl.pallas_call(
        join_kernel,
        in_specs=[VMEM],
        out_specs=VMEM,
        out_shape=jax.ShapeDtypeStruct((rows, count // 2 * cols), F32),
        compiler_params=HELD,
        name="join_pieces",
    )(pieces)


COL_AXES = ("x", "zl")
ROW_AXES = ("c", "zh", "y")
CROP_AXES = ("x", "zl", "c")
GATHER_AXES = ("x", "c")
LAST_AXES = ("x", "c", "zh", "y")
SWAP = [(0, 1), (1, 0)]


def exchange(values, axes):
    return lax.all_to_all(values, axes, 0, 0, tiled=True)


def swap(values, axis):
    return lax.ppermute(values, axis, SWAP)


def pick(values, index):
    return lax.dynamic_index_in_dim(values, index, 0, keepdims=False)


def sum_scatter(stay, go):
    along = lax.axis_index("y")
    half = stay + swap(go, "zh")
    count = half.shape[0]
    total = pick(half, along)
    for step in range(1, count):
        ring = [(i, (i + step) % count) for i in range(count)]
        total = total + lax.ppermute(pick(half, (along + step) % count), "y", ring)
    return total


def on_device(teacher_emb, student_emb, teacher_protos, student_protos):
    core = lax.axis_index("c")
    chip = lax.axis_index(COL_AXES)
    group = lax.axis_index(("zh", "y"))
    chips = lax.axis_size(COL_AXES)
    groups = lax.axis_size(("zh", "y"))
    row_copies = 2 * groups
    shares = lax.axis_size(GATHER_AXES)
    blocks = lax.axis_size("x")
    crops, width = teacher_emb.shape
    batch_total = crops * chips * 2
    proto_total = teacher_protos.shape[1] * groups
    share = lax.axis_index(GATHER_AXES)

    teacher_unit, student_unit, both, place = unit_call(teacher_emb, student_emb)
    teacher_other = swap(teacher_unit, "c")
    gathered = lax.all_gather(both, GATHER_AXES, axis=0, tiled=True)
    student_other = swap(student_unit, "c")

    expo, col_part = teacher_call(place, teacher_unit, teacher_other, teacher_protos)

    near_part = swap(col_part, "zl")
    no_sums = jnp.zeros((1, 2 * crops), F32)
    mixed, sums, dirs, unit = student_call(
        0, place, student_unit, student_other, no_sums, student_protos
    )
    near_part, mixed = lax.optimization_barrier((near_part, mixed))
    col_part = add_call(col_part, near_part)
    col_parts = [
        lax.ppermute(col_part, "x", [(i, (i + step) % blocks) for i in range(blocks)])
        for step in range(1, blocks)
    ]
    student_mixed, total_part, far_dirs, unit = student_call(
        1, place, unit, mixed, sums, student_protos
    )
    col_parts, total_part = lax.optimization_barrier((col_parts, total_part))
    row_part = row_sweep(proto_total, [col_part] + col_parts, expo, row_copies)
    row_parts = exchange(row_part, ROW_AXES)
    col_part = col_sweep(batch_total, row_parts, expo, chips)
    col_parts = exchange(col_part, COL_AXES)
    row_part = row_sweep(proto_total, [col_parts], expo, row_copies, (total_part,))
    row_parts = exchange(row_part, ROW_AXES)
    col_part = col_sweep(batch_total, row_parts, expo, chips)
    col_parts = exchange(col_part, COL_AXES)
    row_part, own_part, other_part, scale = last_sweep(
        proto_total, place, col_parts, expo, dirs, far_dirs, unit, student_mixed,
        blocks * row_copies,
    )
    row_parts = exchange(row_part, LAST_AXES)
    gathered, scale = lax.optimization_barrier((gathered, scale))
    wide_expo, turned, wide_dirs, inverse, wide_mixed = wide_call(
        place, gathered, col_parts, teacher_protos, student_protos, shares, blocks
    )
    far_scale = swap(scale, "c")

    grad_rows, terms = finish_call(
        place, row_parts, col_parts, turned, wide_expo, scale, far_scale, wide_dirs, inverse,
        wide_mixed, 2 * chips,
    )
    loss = (terms + swap(terms, "zl"))[0, 0] / batch_total
    grad_rows = exchange(grad_rows, CROP_AXES)
    grad_prototypes = join_call(grad_rows)

    rows = crops // groups
    far_part, wide_mixed = lax.optimization_barrier((swap(other_part, "c"), wide_mixed))
    pieces = (2, lax.axis_size("y"), rows, 2 * width)
    own_part, far_part = own_part.reshape(pieces), far_part.reshape(pieces)
    summed = sum_scatter(own_part[0] + far_part[0], own_part[1] + far_part[1])
    first = core * crops + group * rows
    sources = lax.dynamic_slice(
        row_parts, (lax.axis_index("x") * row_copies, 0, first), (row_copies, 1, rows)
    )
    row_sum = jnp.sum(sources, axis=(0, 1))
    total = lax.dynamic_slice(
        col_parts, (chip, 0, col_parts.shape[2] - 2 * crops + first), (1, 1, rows)
    ).reshape(rows)
    grad_unit = summed[:, :width] / total[:, None] - summed[:, width:] / row_sum[:, None]
    grad_unit = grad_unit / student_temp
    own_emb = lax.dynamic_slice_in_dim(student_emb, group * rows, rows, 0)
    s_unit, s_norm = unit_rows(own_emb.astype(F32))
    along = jnp.sum(s_unit * grad_unit, axis=1, keepdims=True)
    grad_embeddings = (grad_unit - s_unit * along) / s_norm
    return (grad_embeddings, grad_prototypes, loss)


def solution(mesh):
    fine = Mesh(mesh.devices.reshape(4, 2, 2, 2, 4), ("x", "zl", "c", "zh", "y"))
    crops, protos = ("x", "zl", "c"), ("zh", "y")
    return jax.shard_map(
        on_device,
        mesh=fine,
        in_specs=(P(crops, None), P(crops, None), P(None, protos), P(None, protos)),
        out_specs=(P(crops + protos, None), P(crops, protos), P()),
        check_vma=False,
    )
```
